256 devices in a mesh: inst: 32 (over z, x_lo, core), tp: 8 (over y, x_hi).
Axes of the slice: x: 4 (x_hi: 2, x_lo: 2; x = x_hi * 2 + x_lo), y: 4, z: 8, core: 2. Of those that a mesh axis runs over, the one named last changes fastest.
Arguments:
- queries: bfloat16 [3, 2048, 4096], P(None, 'inst', 'tp'), may hold values from -240 to 240
- incoming_key_value: bfloat16 [3, 2048, 8, 256], P(None, 'inst', 'tp'), may hold values from -6 to 6
- pool: bfloat16 [16384, 8, 16, 256], P('inst', 'tp'), may hold values from -6 to 6
- page_table: int32 [32, 512], P('inst'), may hold values from 0 to 511, each once within a row
- lengths: int32 [32, 64], replicated, may hold values from 1 to 125, as said below
- moving: int32 [3, 32, 8], replicated, may hold values from 0 to 63, as said below
- out_weight: bfloat16 [4096, 4096], P('tp'), may hold values from -0.09375 to 0.09375
Outputs:
- attended: bfloat16 [3, 2048, 4096], P(None, 'inst', 'tp')
- closing_cache: bfloat16 [16384, 8, 16, 256], P('inst', 'tp')
The draws below stay inside these ranges and needn't reach their ends.
Inputs may be any that keep to these rules, and one draw needn't show every extreme that they name: `lengths`: some request in some instance holds exactly 125 tokens. `moving`: for each instance the 24 listed slots are all different.
All inputs are finite; a program needn't handle non-finite values.
Results may differ from the reference program's by a relative error of at most 0.015.
Values may be sent and summed in bfloat16 or wider, within the bound.
No kernel may reach another device: no remote copies, remote signals or barrier semaphores. Data moves between devices by JAX's collectives and lax.ppermute only.
A program may use at most 128 MiB of HBM per device.

```python
import jax
import jax.numpy as jnp
from jax import lax

DM = 4096
QUERY_HEADS = 32
KEY_VALUE_HEADS = 8
HEAD_SIZE = 128
PAGE_TOKENS = 16
DECODE_STEPS = 3
REQUEST_SLOTS = 64
PPS = 8
MIG = 8
POOL_PAGES = 512
INSTANCE_COUNT = 32
LMAX = 125
N_TP = 8


def draw_queries(key, part):
    key = jax.random.fold_in(key, 3)
    first_key = jax.random.fold_in(key, 0)
    base = jnp.clip(jax.random.normal(first_key, (DECODE_STEPS, INSTANCE_COUNT * REQUEST_SLOTS, QUERY_HEADS * HEAD_SIZE), jnp.float32), -6.0, 6.0)
    return base.astype(jnp.bfloat16)


def draw_lengths(key, part):
    key = jax.random.fold_in(key, 1)
    level_key, raw_key, inst_key, slot_key = jax.random.split(key, 4)
    level = jax.random.randint(level_key, (INSTANCE_COUNT, 1), 1, 9)
    raw = jax.random.randint(raw_key, (INSTANCE_COUNT, REQUEST_SLOTS), 0, LMAX)
    counts = 1 + raw * level // 8
    busiest = jax.random.randint(inst_key, (), 0, INSTANCE_COUNT)
    chosen = jax.random.randint(slot_key, (), 0, REQUEST_SLOTS)
    is_hit = (jnp.arange(INSTANCE_COUNT)[:, None] == busiest) & (jnp.arange(REQUEST_SLOTS)[None, :] == chosen)
    return jnp.where(is_hit, LMAX, counts).astype(jnp.int32)


def draw_moving(key, part):
    key = jax.random.fold_in(key, 2)
    inst_keys = jax.random.split(key, INSTANCE_COUNT)

    def pick_slots(one_key):
        return jax.random.permutation(one_key, REQUEST_SLOTS)[:DECODE_STEPS * MIG]
    picked = jax.vmap(pick_slots)(inst_keys)
    return picked.reshape(INSTANCE_COUNT, DECODE_STEPS, MIG).transpose(1, 0, 2).astype(jnp.int32)


def level_of(stream_key, extent, cuts, low, top_value):
    def one(dim, blocks):
        draws = jax.random.uniform(jax.random.fold_in(jax.random.fold_in(stream_key, 6), dim), (blocks,), jnp.float32, low / len(cuts), top_value / len(cuts))
        return jnp.repeat(jnp.exp(draws), extent[dim] // blocks).reshape((-1,) + (1,) * (len(extent) - dim - 1))

    gain = one(*cuts[0])
    for cut in cuts[1:]:
        gain = gain * one(*cut)
    return gain


def noise(stream_key, shape, spread, bound, pieces=(), dtype=jnp.bfloat16):
    entries = jax.random.normal(stream_key, shape, jnp.float32) * spread
    if len(pieces) > 0:
        entries = level_of(stream_key, shape, pieces, -0.22, 0.18) * entries
    return jnp.clip(entries, min=-bound, max=bound).astype(dtype)


def setup_inputs(seed: int = 0) -> dict:
    splits = jax.random.split(jax.random.key(seed), 8)
    return {
        "queries": draw_queries(jax.random.fold_in(splits[7], 71), 0),
        "incoming_key_value": noise(splits[1], (DECODE_STEPS, INSTANCE_COUNT * REQUEST_SLOTS, KEY_VALUE_HEADS, 2 * HEAD_SIZE), 1.0, 6.0, ((1, 32), (2, 8))),
        "pool": noise(splits[2], (INSTANCE_COUNT * POOL_PAGES, KEY_VALUE_HEADS, PAGE_TOKENS, 2 * HEAD_SIZE), 1.0, 6.0, ((0, 32), (1, 8))),
        "page_table": jax.vmap(lambda own: jax.random.permutation(own, POOL_PAGES))(jax.random.split(splits[3], INSTANCE_COUNT)).reshape((INSTANCE_COUNT, POOL_PAGES)).astype(jnp.int32),
        "lengths": draw_lengths(jax.random.fold_in(splits[7], 71), 0),
        "moving": draw_moving(jax.random.fold_in(splits[7], 71), 0),
        "out_weight": noise(splits[6], (QUERY_HEADS * HEAD_SIZE, DM), (QUERY_HEADS * HEAD_SIZE) ** -0.5, 0.09375, ((0, 8),)),
    }


def attend_one(packed):
    pool_one, page_rows, counts, query_vectors = packed
    gathered = pool_one[page_rows].astype(jnp.float32)
    key_part = gathered[..., :HEAD_SIZE]
    value_part = gathered[..., HEAD_SIZE:]
    query_group_width = QUERY_HEADS // KEY_VALUE_HEADS
    grouped_queries = query_vectors.astype(jnp.float32).reshape(REQUEST_SLOTS, KEY_VALUE_HEADS, query_group_width, HEAD_SIZE)
    scores = jnp.einsum("rhgd,rphtd->rhgpt", grouped_queries, key_part) * (HEAD_SIZE ** -0.5)
    position = jnp.arange(PPS)[:, None] * PAGE_TOKENS + jnp.arange(PAGE_TOKENS)[None, :]
    is_live = position[None, None, None] < counts[:, None, None, None, None]
    scores = jnp.where(is_live, scores, -jnp.inf)
    row_max = jnp.max(scores, axis=(3, 4), keepdims=True)
    exp_part = jnp.exp(scores - row_max)
    weights = (exp_part / jnp.sum(exp_part, axis=(3, 4), keepdims=True)).astype(jnp.bfloat16)
    head_out = jnp.einsum("rhgpt,rphtd->rhgd", weights.astype(jnp.float32), value_part)
    return head_out.reshape(REQUEST_SLOTS, QUERY_HEADS * HEAD_SIZE).astype(jnp.bfloat16)


def take_pages(pool_one, page_ids):
    return pool_one[page_ids]


def put_pages(pool_one, page_ids, update):
    return pool_one.at[page_ids].set(update)


def put_counts(counts, slot_ids, update):
    return counts.at[slot_ids].set(update)


def put_token(pool_one, page_ids, offsets, update):
    return pool_one.at[page_ids, :, offsets, :].set(update)


def reference(queries, incoming_key_value, pool, page_table, lengths, moving, out_weight):
    server_instances = lengths.shape[0]
    key_value_page_pool = pool.reshape(server_instances, POOL_PAGES, KEY_VALUE_HEADS, PAGE_TOKENS, 2 * HEAD_SIZE)
    page_map = page_table.reshape(server_instances, REQUEST_SLOTS, PPS)
    counts = lengths
    fresh_tokens_every = incoming_key_value.reshape(DECODE_STEPS, server_instances, REQUEST_SLOTS, KEY_VALUE_HEADS, 2 * HEAD_SIZE)
    asked_all = queries.reshape(DECODE_STEPS, server_instances, REQUEST_SLOTS, QUERY_HEADS * HEAD_SIZE)
    shard_rows = QUERY_HEADS * HEAD_SIZE // N_TP
    results = []
    for step_index in range(DECODE_STEPS):
        distance = server_instances // 2 ** (step_index + 1)
        leaving = moving[step_index]
        page_ids = jnp.take_along_axis(page_map, leaving[:, :, None], axis=1)
        outbox = jax.vmap(take_pages)(key_value_page_pool, page_ids)
        out_counts = jnp.take_along_axis(counts, leaving, axis=1)
        key_value_page_pool = jax.vmap(put_pages)(key_value_page_pool, page_ids, jnp.roll(outbox, distance, axis=0))
        counts = jax.vmap(put_counts)(counts, leaving, jnp.roll(out_counts, distance, axis=0))
        slot_page = jnp.take_along_axis(page_map, (counts // PAGE_TOKENS)[:, :, None], axis=2)[:, :, 0]
        key_value_page_pool = jax.vmap(put_token)(key_value_page_pool, slot_page, counts % PAGE_TOKENS, fresh_tokens_every[step_index])
        counts = counts + 1
        heads = lax.map(attend_one, (key_value_page_pool, page_map, counts, asked_all[step_index]))
        heads = heads.reshape(server_instances * REQUEST_SLOTS, QUERY_HEADS * HEAD_SIZE)
        summed = jnp.zeros((server_instances * REQUEST_SLOTS, DM), jnp.float32)
        for shard in range(N_TP):
            head_term = jnp.dot(heads[:, shard * shard_rows:(shard + 1) * shard_rows],
                                out_weight[shard * shard_rows:(shard + 1) * shard_rows],
                                preferred_element_type=jnp.float32).astype(jnp.bfloat16)
            summed = summed + head_term.astype(jnp.float32)
        results.append(summed.astype(jnp.bfloat16))
    closing_cache = key_value_page_pool.reshape(server_instances * POOL_PAGES, KEY_VALUE_HEADS, PAGE_TOKENS, 2 * HEAD_SIZE)
    return jnp.stack(results), closing_cache
```

```python
import functools

import jax
import jax.numpy as jnp
from jax import lax
from jax.experimental import pallas as pl
from jax.experimental.pallas import tpu as pltpu
from jax.sharding import PartitionSpec as P

F32 = jnp.float32
BF16 = jnp.bfloat16
STEPS = 3
SLOTS = 64
PAGES = 8
TOKENS = 16
MOVES = 8
HEAD = 128
GROUP = 4
ROWS = 16
CHAIN = 6
VMEM_LIMIT = 48 * 1024 * 1024

SMEM_SPEC = pl.BlockSpec(memory_space=pltpu.SMEM)
VMEM_SPEC = pl.BlockSpec(memory_space=pltpu.VMEM)
ANY_SPEC = pl.BlockSpec(memory_space=pl.ANY)


def params():
    return pltpu.CompilerParams(vmem_limit_bytes=VMEM_LIMIT)


def shifted(block, distance):
    count = lax.axis_size("inst")
    return lax.ppermute(
        block, "inst", [((i - distance) % count, i) for i in range(count)]
    )


def with_token(page, token, offset):
    row = lax.broadcasted_iota(jnp.int32, page.shape, 0)
    return jnp.where(row == offset, token.astype(F32), page.astype(F32)).astype(BF16)


def put_tokens(pages, items):
    changed = [with_token(pages[page], token, offset) for page, token, offset in items]
    for (page, _, _), value in zip(items, changed):
        pages[page] = value


def attend(key, value, query, count):
    scores = lax.dot_general(
        query, key, (((1,), (1,)), ((), ())), preferred_element_type=F32
    ) * (HEAD**-0.5)
    lane = lax.broadcasted_iota(jnp.int32, scores.shape, 1)
    step = lax.shift_right_logical(lax.broadcasted_iota(jnp.int32, scores.shape, 0), 2)
    scores = jnp.where(lane - step <= count, scores, -jnp.inf)
    exp_part = jnp.exp(scores - jnp.max(scores, axis=1, keepdims=True))
    weights = exp_part * (1.0 / jnp.sum(exp_part, axis=1, keepdims=True))
    return jnp.dot(weights.astype(BF16), value, preferred_element_type=F32)


def pack_queries_kernel(me_ref, moving, queries, fresh, *rest):
    outs, (natural, packed) = rest[:STEPS], rest[STEPS:]
    me = me_ref[0]
    for step in range(STEPS):
        natural[step, :, : GROUP * HEAD] = queries[step].astype(F32)
        natural[step, :, GROUP * HEAD :] = fresh[step].astype(F32)
    for turn in range(STEPS):
        for m in range(MOVES):
            slot = moving[turn, me, m]
            for step in range(turn, STEPS):
                packed[pl.ds((step - turn) * MOVES + m, 1), :] = natural[
                    step, pl.ds(slot, 1), :
                ]
        count = (STEPS - turn) * MOVES
        outs[turn][...] = packed[:count].astype(BF16)


def pack_queries(me, moving, queries, fresh):
    width = queries.shape[2] + fresh.shape[2]
    return pl.pallas_call(
        pack_queries_kernel,
        out_shape=[
            jax.ShapeDtypeStruct(((STEPS - turn) * MOVES, width), BF16)
            for turn in range(STEPS)
        ],
        in_specs=[SMEM_SPEC] * 2 + [VMEM_SPEC] * 2,
        out_specs=[VMEM_SPEC] * STEPS,
        scratch_shapes=[
            pltpu.VMEM((STEPS, SLOTS, width), F32),
            pltpu.VMEM((STEPS * MOVES, width), F32),
        ],
        compiler_params=params(),
        name="pack_queries",
    )(me, moving, queries, fresh)


def pack_pages_kernel(me_ref, moving, table, lengths, fresh, pool, far, split, mid, near, rows):
    me = me_ref[0]
    for step in range(STEPS):
        rows[step] = fresh[step].astype(F32)
    for turn, targets in enumerate(((far, split), (mid,), (near,))):
        start = 0
        for target in targets:
            for m in range(target.shape[0] // PAGES):
                slot = moving[turn, me, start + m]
                for page in range(PAGES):
                    target[m * PAGES + page] = pool[table[0, slot * PAGES + page]]
            start += target.shape[0] // PAGES
    for turn, target in ((1, mid), (2, near)):
        for step in range(turn):
            items = []
            for m in range(MOVES):
                slot = moving[turn, me, m]
                position = lengths[me, slot] + step
                items.append(
                    (
                        m * PAGES + lax.shift_right_logical(position, 4),
                        rows[step, pl.ds(slot, 1), :],
                        position & (TOKENS - 1),
                    )
                )
            put_tokens(target, items)


def pack_pages(me, moving, table, lengths, fresh, pool):
    page = pool.shape[1:]
    counts = (CHAIN, MOVES - CHAIN, MOVES, MOVES)
    return pl.pallas_call(
        pack_pages_kernel,
        out_shape=[jax.ShapeDtypeStruct((n * PAGES,) + page, BF16) for n in counts],
        in_specs=[SMEM_SPEC] * 4 + [VMEM_SPEC] * 2,
        out_specs=[VMEM_SPEC] * len(counts),
        scratch_shapes=[pltpu.VMEM((STEPS, SLOTS, 2 * HEAD), F32)],
        compiler_params=params(),
        name="pack_pages",
    )(me, moving, table, lengths, fresh, pool)


def attend_moved_kernel(me_ref, moving, lengths, far, split, mid, near, *rest):
    asked, outs, (pages, query, result, rows) = rest[:3], rest[3:6], rest[6:]
    me = me_ref[0]
    per_turn = MOVES * PAGES
    pages[: CHAIN * PAGES] = far[...]
    pages[CHAIN * PAGES : per_turn] = split[...]
    pages[per_turn : 2 * per_turn] = mid[...]
    pages[2 * per_turn :] = near[...]
    query[...] = jnp.zeros_like(query)
    for turn in range(STEPS):
        for step in range(turn, STEPS):
            block = asked[turn][
                (step - turn) * MOVES : (step - turn + 1) * MOVES, :
            ].astype(F32)
            for head in range(GROUP):
                query[
                    turn * MOVES : (turn + 1) * MOVES, step * GROUP + head, :
                ] = block[:, head * HEAD : (head + 1) * HEAD]
            rows[...] = block[:, GROUP * HEAD :]
            items = []
            for m in range(MOVES):
                position = lengths[me, moving[turn, me, m]] + step
                items.append(
                    (
                        turn * per_turn
                        + m * PAGES
                        + lax.shift_right_logical(position, 4),
                        rows[m : m + 1, :],
                        position & (TOKENS - 1),
                    )
                )
            put_tokens(pages, items)

    @pl.loop(0, STEPS)
    def _(turn):
        for m in range(MOVES):
            index = turn * MOVES + m
            both = pages[pl.ds(index * PAGES, PAGES)].reshape(PAGES * TOKENS, 2 * HEAD)
            result[index] = attend(
                both[:, :HEAD],
                both[:, HEAD:],
                query[index].astype(BF16),
                lengths[me, moving[turn, me, m]],
            )

    for turn in range(STEPS):
        for step in range(turn, STEPS):
            for head in range(GROUP):
                outs[turn][
                    (step - turn) * MOVES : (step - turn + 1) * MOVES,
                    head * HEAD : (head + 1) * HEAD,
                ] = result[
                    turn * MOVES : (turn + 1) * MOVES, step * GROUP + head, :
                ].astype(BF16)


def attend_moved(me, moving, lengths, blocks, asked):
    page = blocks[0].shape[1:]
    return pl.pallas_call(
        attend_moved_kernel,
        out_shape=[
            jax.ShapeDtypeStruct(((STEPS - turn) * MOVES, GROUP * HEAD), BF16)
            for turn in range(STEPS)
        ],
        in_specs=[SMEM_SPEC] * 3 + [VMEM_SPEC] * 7,
        out_specs=[VMEM_SPEC] * STEPS,
        scratch_shapes=[
            pltpu.VMEM((STEPS * MOVES * PAGES,) + page, BF16),
            pltpu.VMEM((STEPS * MOVES, ROWS, HEAD), F32),
            pltpu.VMEM((STEPS * MOVES, ROWS, HEAD), F32),
            pltpu.VMEM((MOVES, 2 * HEAD), F32),
        ],
        compiler_params=params(),
        name="attend_moved",
    )(me, moving, lengths, *blocks, *asked)


def attend_local_kernel(
    me_ref, table, lengths, queries, fresh, pool, heads, cache, pages, query, result, rows, sem
):
    me = me_ref[0]
    load = pltpu.make_async_copy(pool, pages, sem)
    load.start()
    query[...] = jnp.zeros_like(query)
    for step in range(STEPS):
        rows[step] = fresh[step].astype(F32)
        for head in range(GROUP):
            query[:, step * GROUP + head, :] = queries[
                step, :, head * HEAD : (head + 1) * HEAD
            ].astype(F32)
    load.wait()

    @pl.loop(0, SLOTS // MOVES)
    def _(block):
        slots = [block * MOVES + m for m in range(MOVES)]
        held = [lengths[me, slot] for slot in slots]
        for step in range(STEPS):
            items = []
            for slot, length in zip(slots, held):
                position = length + step
                page = table[0, slot * PAGES + lax.shift_right_logical(position, 4)]
                items.append(
                    (page, rows[step, pl.ds(slot, 1), :], position & (TOKENS - 1))
                )
            put_tokens(pages, items)

    store = pltpu.make_async_copy(pages, cache, sem)
    store.start()

    @pl.loop(0, SLOTS // MOVES)
    def _(block):
        for m in range(MOVES):
            slot = block * MOVES + m
            both = jnp.concatenate(
                [pages[table[0, slot * PAGES + page]] for page in range(PAGES)], axis=0
            )
            result[slot] = attend(
                both[:, :HEAD], both[:, HEAD:], query[slot].astype(BF16), lengths[me, slot]
            )

    for step in range(STEPS):
        for head in range(GROUP):
            heads[step, :, head * HEAD : (head + 1) * HEAD] = result[
                :, step * GROUP + head, :
            ].astype(BF16)
    store.wait()


def attend_local(me, table, lengths, queries, fresh, pool):
    return pl.pallas_call(
        attend_local_kernel,
        out_shape=[
            jax.ShapeDtypeStruct(queries.shape, BF16),
            jax.ShapeDtypeStruct(pool.shape, BF16),
        ],
        in_specs=[SMEM_SPEC] * 3 + [VMEM_SPEC] * 2 + [ANY_SPEC],
        out_specs=[VMEM_SPEC, ANY_SPEC],
        scratch_shapes=[
            pltpu.VMEM(pool.shape, BF16),
            pltpu.VMEM((SLOTS, ROWS, HEAD), F32),
            pltpu.VMEM((SLOTS, ROWS, HEAD), F32),
            pltpu.VMEM((STEPS, SLOTS, 2 * HEAD), F32),
            pltpu.SemaphoreType.DMA,
        ],
        compiler_params=params(),
        name="attend_local",
    )(me, table, lengths, queries, fresh, pool)


def project_kernel(me_ref, moving, heads, far, mid, near, weight, out, natural, whole):
    me = me_ref[0]

    @pl.when(pl.program_id(0) == 0)
    def _():
        for step in range(STEPS):
            natural[step * SLOTS : (step + 1) * SLOTS, :] = heads[step].astype(F32)
        for turn, back in enumerate((far, mid, near)):
            block = back[...].astype(F32)
            for m in range(MOVES):
                slot = moving[turn, me, m]
                for step in range(turn, STEPS):
                    k = (step - turn) * MOVES + m
                    natural[pl.ds(step * SLOTS + slot, 1), :] = block[k : k + 1, :]
        whole[...] = natural[...].astype(BF16)

    out[0] = jnp.dot(whole[...], weight[...], preferred_element_type=F32).astype(BF16)


def project(me, moving, heads, back, weight, parts):
    depth, width = weight.shape
    column = width // parts
    rows = STEPS * SLOTS

    def fixed(shape):
        return pl.BlockSpec(shape, lambda i: (0,) * len(shape))

    return pl.pallas_call(
        project_kernel,
        grid=(parts,),
        out_shape=jax.ShapeDtypeStruct((parts, rows, column), BF16),
        in_specs=[SMEM_SPEC] * 2
        + [fixed(heads.shape)]
        + [fixed(b.shape) for b in back]
        + [pl.BlockSpec((depth, column), lambda i: (0, i))],
        out_specs=pl.BlockSpec((1, rows, column), lambda i: (i, 0, 0)),
        scratch_shapes=[
            pltpu.VMEM((rows, depth), F32),
            pltpu.VMEM((rows, depth), BF16),
        ],
        compiler_params=params(),
        name="project",
    )(me, moving, heads, *back, weight)


def store_pages_kernel(
    turn, first, hop, me_ref, moving, table, lengths, fresh, arrived, cache_in, cache, pages, rows, sem
):
    me = me_ref[0]
    count = lengths.shape[0]
    source = lax.rem(me - hop + count, count)
    pages[...] = arrived[...]
    for step in range(turn, STEPS):
        rows[step] = fresh[step].astype(F32)
    moves = arrived.shape[0] // PAGES
    for step in range(turn, STEPS):
        items = []
        for m in range(moves):
            slot = moving[turn, me, first + m]
            position = lengths[source, moving[turn, source, first + m]] + step
            items.append(
                (
                    m * PAGES + lax.shift_right_logical(position, 4),
                    rows[step, pl.ds(slot, 1), :],
                    position & (TOKENS - 1),
                )
            )
        put_tokens(pages, items)
    for m in range(moves):
        slot = moving[turn, me, first + m]
        for page in range(PAGES):
            pltpu.make_async_copy(
                pages.at[m * PAGES + page],
                cache.at[table[0, slot * PAGES + page]],
                sem,
            ).start()
    pltpu.make_async_copy(pages, cache.at[pl.ds(0, moves * PAGES)], sem).wait()


def store_pages(turn, first, hop, me, moving, table, lengths, fresh, arrived, cache):
    return pl.pallas_call(
        functools.partial(store_pages_kernel, turn, first, hop),
        out_shape=jax.ShapeDtypeStruct(cache.shape, BF16),
        in_specs=[SMEM_SPEC] * 4 + [VMEM_SPEC] * 2 + [ANY_SPEC],
        out_specs=ANY_SPEC,
        scratch_shapes=[
            pltpu.VMEM(arrived.shape, BF16),
            pltpu.VMEM((STEPS, SLOTS, 2 * HEAD), F32),
            pltpu.SemaphoreType.DMA,
        ],
        input_output_aliases={6: 0},
        compiler_params=params(),
        name="store_pages",
    )(me, moving, table, lengths, fresh, arrived, cache)


def shards(queries, incoming, pool, table, lengths, moving, weight):
    count = lax.axis_size("inst")
    parts = lax.axis_size("tp")
    me = lax.axis_index("inst").reshape(1)
    hops = [count // 2 ** (step + 1) for step in range(STEPS)]
    fresh = incoming.reshape(STEPS, SLOTS, 2 * HEAD)
    own = pool.reshape(pool.shape[0], TOKENS, 2 * HEAD)

    asked = pack_queries(me, moving, queries, fresh)
    asked = [shifted(block, -hop) for block, hop in zip(asked, hops)]
    far, split, mid, near = pack_pages(me, moving, table, lengths, fresh, own)
    near_in = shifted(near, hops[2])
    far_half = shifted(far, -hops[1])
    mid_in = shifted(mid, hops[1])
    split_in = shifted(split, hops[0])

    back = attend_moved(me, moving, lengths, (far, split, mid, near), asked)
    back = [shifted(block, hop) for block, hop in zip(back, hops)]
    heads, cache = attend_local(me, table, lengths, queries, fresh, own)
    far_in = shifted(far_half, -hops[1])
    partial = project(me, moving, heads, back, weight, parts)
    partial = lax.all_to_all(partial, "tp", 0, 0, tiled=True)
    attended = jnp.sum(partial.astype(F32), axis=0).astype(BF16)

    for turn, first, arrived in (
        (2, 0, near_in),
        (1, 0, mid_in),
        (0, CHAIN, split_in),
        (0, 0, far_in),
    ):
        cache = store_pages(
            turn, first, hops[turn], me, moving, table, lengths, fresh, arrived, cache
        )
    return attended.reshape(queries.shape), cache.reshape(pool.shape)


def solution(mesh):
    placed = (
        P(None, "inst", "tp"),
        P(None, "inst", "tp", None),
        P("inst", "tp", None, None),
        P("inst", None),
        P(),
        P(),
        P("tp", None),
    )
    return jax.shard_map(
        shards,
        mesh=mesh,
        in_specs=placed,
        out_specs=(P(None, "inst", "tp"), P("inst", "tp", None, None)),
        check_vma=False,
    )
```

```python
import functools

import jax
import jax.numpy as jnp
from jax import lax
from jax.experimental import pallas as pl
from jax.experimental.pallas import tpu as pltpu
from jax.sharding import PartitionSpec as P

F32 = jnp.float32
BF16 = jnp.bfloat16
STEPS = 3
SLOTS = 64
PAGES = 8
TOKENS = 16
MOVES = 8
HEAD = 128
GROUP = 4
ROWS = 16
CHUNKS = 8
KEPT = tuple(SLOTS - MOVES * (step + 1) for step in range(STEPS))
BATCH = 16
VMEM_MOST = 61 * 1024 * 1024
VMEM_SOME = 20 * 1024 * 1024

SMEM_SPEC = pl.BlockSpec(memory_space=pltpu.SMEM)
VMEM_SPEC = pl.BlockSpec(memory_space=pltpu.VMEM)
ANY_SPEC = pl.BlockSpec(memory_space=pl.ANY)
HBM_SPEC = pl.BlockSpec(memory_space=pltpu.HBM)


def params(limit=VMEM_SOME):
    return pltpu.CompilerParams(vmem_limit_bytes=limit)


def cost():
    return pl.CostEstimate(flops=1, bytes_accessed=1, transcendentals=0)


def fetch(pairs, sems):
    copies = [
        pltpu.make_async_copy(source, target, sems.at[k])
        for k, (source, target) in enumerate(pairs)
    ]
    for copy in copies:
        copy.start()
    return copies


def shifted(block, distance):
    count = lax.axis_size("inst")
    return lax.ppermute(
        block, "inst", [((i - distance) % count, i) for i in range(count)]
    )


def with_token(page, token, offset):
    row = lax.broadcasted_iota(jnp.int32, page.shape, 0)
    return jnp.where(row == offset, token.astype(F32), page.astype(F32)).astype(BF16)


def put_tokens(pages, items):
    changed = [with_token(pages[page], token, offset) for page, token, offset in items]
    for (page, _, _), value in zip(items, changed):
        pages[page] = value


def parts_of(source, target):
    size = source.shape[0] // CHUNKS
    return [
        (source.at[pl.ds(k * size, size)], target.at[pl.ds(k * size, size)])
        for k in range(CHUNKS)
    ]


def attend_block(pages, queries, counts):
    scores = jnp.concatenate(
        [
            lax.dot_general(
                query,
                page[:, :HEAD],
                (((1,), (1,)), ((), ())),
                preferred_element_type=F32,
            )
            for page, query in zip(pages, queries)
        ],
        axis=0,
    ) * (HEAD**-0.5)
    lane = lax.broadcasted_iota(jnp.int32, (ROWS, HEAD), 1)
    step = lax.shift_right_logical(lax.broadcasted_iota(jnp.int32, (ROWS, HEAD), 0), 2)
    lag = lane - step
    live = jnp.concatenate([lag - count for count in counts], axis=0) <= 0
    scores = jnp.where(live, scores, -jnp.inf)
    exp_part = jnp.exp(scores - jnp.max(scores, axis=1, keepdims=True))
    weights = exp_part * (1.0 / jnp.sum(exp_part, axis=1, keepdims=True))
    weights = weights.astype(BF16)
    return [
        jnp.dot(
            weights[i * ROWS : (i + 1) * ROWS],
            page[:, HEAD:],
            preferred_element_type=F32,
        )
        for i, page in enumerate(pages)
    ]


def pack_kernel(me_ref, moving_in, table_in, lengths_in, fresh_in, pool_in, *rest):
    (far, both), rest = rest[:2], rest[2:]
    moving, table, lengths, fresh, pool, rows, sems = rest
    loads = fetch(
        (
            (moving_in, moving),
            (table_in, table),
            (lengths_in, lengths),
            (fresh_in, fresh),
            *parts_of(pool_in, pool),
        ),
        sems,
    )
    me = me_ref[0]
    for load in loads[:4]:
        load.wait()
    for step in range(STEPS):
        rows[step] = fresh[step].astype(F32)
    for load in loads[4:]:
        load.wait()
    for turn, target, start in ((0, far, 0), (2, both, 0), (1, both, MOVES)):
        for m in range(MOVES):
            slot = moving[turn, m, me]
            for page in range(PAGES):
                target[(start + m) * PAGES + page] = pool[table[0, slot * PAGES + page]]
        for step in range(turn):
            items = []
            for m in range(MOVES):
                slot = moving[turn, m, me]
                position = lengths[me, slot] + step
                items.append(
                    (
                        (start + m) * PAGES + lax.shift_right_logical(position, 4),
                        rows[step, pl.ds(slot, 1), :],
                        position & (TOKENS - 1),
                    )
                )
            put_tokens(target, items)


def pack(me, moving, table, lengths, fresh, pool):
    return pl.pallas_call(
        pack_kernel,
        out_shape=[
            jax.ShapeDtypeStruct((size * PAGES,) + pool.shape[1:], BF16)
            for size in (MOVES, 2 * MOVES)
        ],
        in_specs=[SMEM_SPEC] + [HBM_SPEC] * 5,
        out_specs=[VMEM_SPEC] * 2,
        scratch_shapes=[
            pltpu.SMEM(moving.shape, jnp.int32),
            pltpu.SMEM(table.shape, jnp.int32),
            pltpu.SMEM(lengths.shape, jnp.int32),
            pltpu.VMEM(fresh.shape, BF16),
            pltpu.VMEM(pool.shape, BF16),
            pltpu.VMEM(fresh.shape, F32),
            pltpu.SemaphoreType.DMA((4 + CHUNKS,)),
        ],
        compiler_params=params(VMEM_MOST),
        cost_estimate=cost(),
        name="pack",
    )(me, moving, table, lengths, fresh, pool)


def gathered(pages, table, slot):
    return jnp.concatenate(
        [pages[table[0, slot * PAGES + page]] for page in range(PAGES)], axis=0
    )


def attend_local_kernel(
    me_ref, table, lengths, queries, fresh, pool, heads, cache, pages, query, result, rows, sems
):
    me = me_ref[0]
    loads = fetch(parts_of(pool, pages), sems)
    query[...] = jnp.zeros_like(query)
    for step in range(STEPS):
        rows[step] = fresh[step].astype(F32)
        for head in range(GROUP):
            query[:, step * GROUP + head, :] = queries[
                step, :, head * HEAD : (head + 1) * HEAD
            ].astype(F32)
    for load in loads:
        load.wait()

    @pl.loop(0, SLOTS // MOVES)
    def _(block):
        slots = [block * MOVES + m for m in range(MOVES)]
        held = [lengths[me, slot] for slot in slots]
        for step in range(STEPS):
            items = []
            for slot, length in zip(slots, held):
                position = length + step
                page = table[0, slot * PAGES + lax.shift_right_logical(position, 4)]
                items.append(
                    (page, rows[step, pl.ds(slot, 1), :], position & (TOKENS - 1))
                )
            put_tokens(pages, items)

    stores = fetch(parts_of(pages, cache), sems)

    @pl.loop(0, SLOTS // BATCH)
    def _(block):
        slots = [block * BATCH + m for m in range(BATCH)]
        out = attend_block(
            [gathered(pages, table, slot) for slot in slots],
            [query[slot].astype(BF16) for slot in slots],
            [lengths[me, slot] for slot in slots],
        )
        for slot, value in zip(slots, out):
            result[slot] = value

    for step in range(STEPS):
        for head in range(GROUP):
            heads[step, :, head * HEAD : (head + 1) * HEAD] = result[
                :, step * GROUP + head, :
            ].astype(BF16)
    for store in stores:
        store.wait()


def attend_local(me, table, lengths, queries, fresh, pool):
    return pl.pallas_call(
        attend_local_kernel,
        out_shape=[
            jax.ShapeDtypeStruct(queries.shape, BF16),
            jax.ShapeDtypeStruct(pool.shape, BF16),
        ],
        in_specs=[SMEM_SPEC] * 3 + [VMEM_SPEC] * 2 + [ANY_SPEC],
        out_specs=[VMEM_SPEC, ANY_SPEC],
        scratch_shapes=[
            pltpu.VMEM(pool.shape, BF16),
            pltpu.VMEM((SLOTS, ROWS, HEAD), F32),
            pltpu.VMEM((SLOTS, ROWS, HEAD), F32),
            pltpu.VMEM((STEPS, SLOTS, 2 * HEAD), F32),
            pltpu.SemaphoreType.DMA((CHUNKS,)),
        ],
        compiler_params=params(VMEM_MOST),
        cost_estimate=cost(),
        name="attend_local",
    )(me, table, lengths, queries, fresh, pool)


def mark_slots(marks, moving, me):
    for slot in range(SLOTS):
        marks[slot] = STEPS
    for turn in range(STEPS):
        for m in range(MOVES):
            marks[moving[turn, m, me]] = turn


def project_kernel(me_ref, moving, heads, weight, out, weights, natural, packed, marks, sems):
    parts = weights.shape[0]
    column = weights.shape[2]
    loads = fetch(
        [
            (weight.at[:, pl.ds(part * column, column)], weights.at[part])
            for part in range(parts)
        ],
        sems,
    )
    mark_slots(marks, moving, me_ref[0])
    start = 0
    for step in range(STEPS):
        natural[...] = heads[step].astype(F32)
        row = start
        for slot in range(SLOTS):
            packed[pl.ds(row, 1), :] = natural[slot : slot + 1, :]
            row = row + (marks[slot] > step).astype(jnp.int32)
        start += KEPT[step]
    whole = packed[:start].astype(BF16)
    for part, load in enumerate(loads):
        load.wait()
        out[part] = jnp.dot(
            whole, weights[part], preferred_element_type=F32
        ).astype(BF16)


def project(me, moving, heads, weight, parts):
    depth, width = weight.shape
    rows = sum(KEPT)
    column = width // parts
    return pl.pallas_call(
        project_kernel,
        out_shape=jax.ShapeDtypeStruct((parts, rows, column), BF16),
        in_specs=[SMEM_SPEC] * 2 + [VMEM_SPEC] + [ANY_SPEC],
        out_specs=VMEM_SPEC,
        scratch_shapes=[
            pltpu.VMEM((parts, depth, column), BF16),
            pltpu.VMEM((SLOTS, depth), F32),
            pltpu.VMEM((rows + 8, depth), F32),
            pltpu.SMEM((SLOTS,), jnp.int32),
            pltpu.SemaphoreType.DMA((parts,)),
        ],
        compiler_params=params(VMEM_MOST),
        cost_estimate=cost(),
        name="project",
    )(me, moving, heads, weight)


def attend_taken_kernel(
    turns, pieces, hops, final, me_ref, moving, table, lengths, queries, fresh, *rest
):
    taken = len(turns)
    arrived, rest = rest[: len(pieces)], rest[len(pieces) :]
    pages, natural, query, result, row_list, sem = rest[-6:]
    rest = rest[:-6]
    if final:
        earlier, weight, _, out, cache, weights, weight_sems = rest
        parts = weights.shape[0]
        column = weights.shape[2]
        loads = fetch(
            [
                (weight.at[:, pl.ds(part * column, column)], weights.at[part])
                for part in range(parts)
            ],
            weight_sems,
        )
    else:
        _, out, cache = rest
    me = me_ref[0]
    width = GROUP * HEAD
    block = MOVES * PAGES
    instances = lengths.shape[0]
    query[...] = jnp.zeros_like(query)
    for step in range(min(turns), STEPS):
        natural[step, :, :width] = queries[step].astype(F32)
        natural[step, :, width:] = fresh[step].astype(F32)
    for (start, size), piece in zip(pieces, arrived):
        pages[start : start + size] = piece[:size]
    counts = []
    for i, turn in enumerate(turns):
        source = lax.rem(me - hops[turn] + instances, instances)
        slots = [moving[turn, m, me] for m in range(MOVES)]
        held = [lengths[source, moving[turn, m, source]] for m in range(MOVES)]
        counts += held
        for step in range(turn, STEPS):
            for m in range(MOVES):
                row_list[m : m + 1, :] = natural[step, pl.ds(slots[m], 1), :]
            for head in range(GROUP):
                query[i * MOVES : (i + 1) * MOVES, step * GROUP + head, :] = row_list[
                    :, head * HEAD : (head + 1) * HEAD
                ]
            put_tokens(
                pages,
                [
                    (
                        i * block + m * PAGES + lax.shift_right_logical(held[m] + step, 4),
                        row_list[m : m + 1, width:],
                        (held[m] + step) & (TOKENS - 1),
                    )
                    for m in range(MOVES)
                ],
            )
        for m in range(MOVES):
            for page in range(PAGES):
                pltpu.make_async_copy(
                    pages.at[i * block + m * PAGES + page],
                    cache.at[table[0, slots[m] * PAGES + page]],
                    sem,
                ).start()
    values = attend_block(
        [
            pages[i * PAGES : (i + 1) * PAGES].reshape(PAGES * TOKENS, 2 * HEAD)
            for i in range(taken * MOVES)
        ],
        [query[i].astype(BF16) for i in range(taken * MOVES)],
        counts,
    )
    for i, value in enumerate(values):
        result[i] = value
    found = []
    for i, turn in enumerate(turns):
        for step in range(turn, STEPS):
            found.append(
                jnp.concatenate(
                    [
                        result[i * MOVES : (i + 1) * MOVES, step * GROUP + head, :]
                        for head in range(GROUP)
                    ],
                    axis=1,
                )
            )
    if final:
        whole = jnp.concatenate(found + [earlier[...]], axis=0).astype(BF16)
        for part, load in enumerate(loads):
            load.wait()
            out[part] = jnp.dot(
                whole, weights[part], preferred_element_type=F32
            ).astype(BF16)
    else:
        out[...] = jnp.concatenate(found, axis=0)
    pltpu.make_async_copy(pages, cache.at[pl.ds(0, taken * block)], sem).wait()


def attend_taken(
    turns, pieces, hops, me, moving, table, lengths, queries, fresh, arrived, cache, final=None
):
    taken = len(turns)
    width = queries.shape[2] + fresh.shape[2]
    rows = sum(STEPS - turn for turn in turns) * MOVES
    in_specs = [SMEM_SPEC] * 4 + [VMEM_SPEC] * (2 + len(arrived))
    operands = [me, moving, table, lengths, queries, fresh, *arrived]
    extra = []
    out = jax.ShapeDtypeStruct((rows, queries.shape[2]), F32)
    if final is not None:
        earlier, weight, parts = final
        in_specs += [VMEM_SPEC, ANY_SPEC]
        operands += [earlier, weight]
        column = weight.shape[1] // parts
        extra = [
            pltpu.VMEM((parts, weight.shape[0], column), BF16),
            pltpu.SemaphoreType.DMA((parts,)),
        ]
        out = jax.ShapeDtypeStruct((parts, rows + earlier.shape[0], column), BF16)
    return pl.pallas_call(
        functools.partial(attend_taken_kernel, turns, pieces, hops, final is not None),
        out_shape=[out, jax.ShapeDtypeStruct(cache.shape, BF16)],
        in_specs=in_specs + [ANY_SPEC],
        out_specs=[VMEM_SPEC, ANY_SPEC],
        scratch_shapes=extra
        + [
            pltpu.VMEM((taken * MOVES * PAGES,) + cache.shape[1:], BF16),
            pltpu.VMEM((STEPS, SLOTS, width), F32),
            pltpu.VMEM((taken * MOVES, ROWS, HEAD), F32),
            pltpu.VMEM((taken * MOVES, ROWS, HEAD), F32),
            pltpu.VMEM((MOVES, width), F32),
            pltpu.SemaphoreType.DMA,
        ],
        input_output_aliases={len(operands): 1},
        compiler_params=params(),
        cost_estimate=cost(),
        name="attend_taken",
    )(*operands, cache)


def summed(blocks):
    total = blocks[0].astype(F32)
    for part in range(1, blocks.shape[0]):
        total = total + blocks[part].astype(F32)
    return total


def assemble_kernel(order, me_ref, moving, local, late, out, rows, kept, taken, marks):
    me = me_ref[0]
    mark_slots(marks, moving, me)
    kept[: local.shape[1]] = summed(local)
    row = 0
    for step in range(STEPS):
        index = row
        for slot in range(SLOTS):
            rows[step * SLOTS + slot : step * SLOTS + slot + 1, :] = kept[
                pl.ds(index, 1), :
            ]
            index = index + (marks[slot] > step).astype(jnp.int32)
        row += KEPT[step]
    taken[...] = summed(late)
    row = 0
    for turn in order:
        for step in range(turn, STEPS):
            for m in range(MOVES):
                rows[pl.ds(step * SLOTS + moving[turn, m, me], 1), :] = taken[
                    row : row + 1, :
                ]
                row += 1
    out[...] = rows[...].astype(BF16)


def assemble(order, me, moving, local, late):
    column = local.shape[2]
    rows = STEPS * SLOTS
    return pl.pallas_call(
        functools.partial(assemble_kernel, order),
        out_shape=jax.ShapeDtypeStruct((rows, column), BF16),
        in_specs=[SMEM_SPEC] * 2 + [VMEM_SPEC] * 2,
        out_specs=VMEM_SPEC,
        scratch_shapes=[
            pltpu.VMEM((rows, column), F32),
            pltpu.VMEM((local.shape[1] + 8, column), F32),
            pltpu.VMEM((late.shape[1], column), F32),
            pltpu.SMEM((SLOTS,), jnp.int32),
        ],
        compiler_params=params(),
        cost_estimate=cost(),
        name="assemble",
    )(me, moving, local, late)


def shards(queries, incoming, pool, table, lengths, moving, weight):
    count = lax.axis_size("inst")
    parts = lax.axis_size("tp")
    me = lax.axis_index("inst").reshape(1)
    hops = tuple(count // 2 ** (step + 1) for step in range(STEPS))
    fresh = incoming.reshape(STEPS, SLOTS, 2 * HEAD)
    own = pool.reshape(pool.shape[0], TOKENS, 2 * HEAD)

    moving = moving.transpose(0, 2, 1)
    far, both = pack(me, moving, table, lengths, fresh, own)
    block = MOVES * PAGES
    far_half = shifted(far, -hops[1])
    both_in = shifted(both, hops[2])
    heads, cache = attend_local(me, table, lengths, queries, fresh, own)
    local = project(me, moving, heads, weight, parts)
    local = lax.all_to_all(local, "tp", 0, 0, tiled=True)
    far_in = shifted(far_half, -hops[1])
    mid_in = shifted(both_in[block:], hops[1] - hops[2])

    common = (hops, me, moving, table, lengths, queries, fresh)
    found, cache = attend_taken(
        (1, 2), ((0, block), (block, block)), *common, (mid_in, both_in), cache
    )
    late, cache = attend_taken(
        (0,),
        ((0, block),),
        *common,
        (far_in,),
        cache,
        (found, weight, parts),
    )
    late = lax.all_to_all(late, "tp", 0, 0, tiled=True)
    attended = assemble((0, 1, 2), me, moving, local, late)
    return attended.reshape(queries.shape), cache.reshape(pool.shape)


def solution(mesh):
    placed = (
        P(None, "inst", "tp"),
        P(None, "inst", "tp", None),
        P("inst", "tp", None, None),
        P("inst", None),
        P(),
        P(),
        P("tp", None),
    )
    return jax.shard_map(
        shards,
        mesh=mesh,
        in_specs=placed,
        out_specs=(P(None, "inst", "tp"), P("inst", "tp", None, None)),
        check_vma=False,
    )
```

```python
import functools

import jax
import jax.numpy as jnp
from jax import lax
from jax.experimental import pallas as pl
from jax.experimental.pallas import tpu as pltpu
from jax.sharding import PartitionSpec as P

F32 = jnp.float32
BF16 = jnp.bfloat16
STEPS = 3
SLOTS = 64
PAGES = 8
TOKENS = 16
MOVES = 8
HEAD = 128
GROUP = 4
ROWS = 16
CHUNKS = 8
KEPT = tuple(SLOTS - MOVES * (step + 1) for step in range(STEPS))
MOVED = tuple(MOVES * (STEPS - turn) for turn in range(STEPS))
BATCH = 16
VMEM_MOST = 61 * 1024 * 1024
VMEM_SOME = 20 * 1024 * 1024

SMEM_SPEC = pl.BlockSpec(memory_space=pltpu.SMEM)
VMEM_SPEC = pl.BlockSpec(memory_space=pltpu.VMEM)
ANY_SPEC = pl.BlockSpec(memory_space=pl.ANY)
HBM_SPEC = pl.BlockSpec(memory_space=pltpu.HBM)


def params(limit=VMEM_SOME):
    return pltpu.CompilerParams(vmem_limit_bytes=limit)


def cost():
    return pl.CostEstimate(flops=1, bytes_accessed=1, transcendentals=0)


def fetch(pairs, sems):
    copies = [
        pltpu.make_async_copy(source, target, sems.at[k])
        for k, (source, target) in enumerate(pairs)
    ]
    for copy in copies:
        copy.start()
    return copies


def shifted(block, distance):
    count = lax.axis_size("inst")
    return lax.ppermute(
        block, "inst", [((i - distance) % count, i) for i in range(count)]
    )


def with_token(page, token, offset):
    row = lax.broadcasted_iota(jnp.int32, page.shape, 0)
    return jnp.where(row == offset, token.astype(F32), page.astype(F32)).astype(BF16)


def put_tokens(pages, items):
    changed = [with_token(pages[page], token, offset) for page, token, offset in items]
    for (page, _, _), value in zip(items, changed):
        pages[page] = value


def parts_of(source, target):
    size = source.shape[0] // CHUNKS
    return [
        (source.at[pl.ds(k * size, size)], target.at[pl.ds(k * size, size)])
        for k in range(CHUNKS)
    ]


def attend_block(pages, queries, counts):
    scores = jnp.concatenate(
        [
            lax.dot_general(
                query,
                page[:, :HEAD],
                (((1,), (1,)), ((), ())),
                preferred_element_type=F32,
            )
            for page, query in zip(pages, queries)
        ],
        axis=0,
    ) * (HEAD**-0.5)
    lane = lax.broadcasted_iota(jnp.int32, (ROWS, HEAD), 1)
    step = lax.shift_right_logical(lax.broadcasted_iota(jnp.int32, (ROWS, HEAD), 0), 2)
    lag = lane - step
    live = jnp.concatenate([lag - count for count in counts], axis=0) <= 0
    scores = jnp.where(live, scores, -jnp.inf)
    exp_part = jnp.exp(scores - jnp.max(scores, axis=1, keepdims=True))
    weights = exp_part * (1.0 / jnp.sum(exp_part, axis=1, keepdims=True))
    weights = weights.astype(BF16)
    return [
        jnp.dot(
            weights[i * ROWS : (i + 1) * ROWS],
            page[:, HEAD:],
            preferred_element_type=F32,
        )
        for i, page in enumerate(pages)
    ]


def pack_queries_kernel(me_ref, moving_in, queries_in, fresh_in, *rest):
    outs, (moving, queries, fresh, natural, packed, sems) = rest[:STEPS], rest[STEPS:]
    loads = fetch(
        ((moving_in, moving), (queries_in, queries), (fresh_in, fresh)), sems
    )
    me = me_ref[0]
    width = GROUP * HEAD
    for load in loads:
        load.wait()
    for step in range(STEPS):
        natural[step, :, :width] = queries[step].astype(F32)
        natural[step, :, width:] = fresh[step].astype(F32)
    for turn in range(STEPS):
        for m in range(MOVES):
            slot = moving[turn, m, me]
            for step in range(turn, STEPS):
                packed[pl.ds((step - turn) * MOVES + m, 1), :] = natural[
                    step, pl.ds(slot, 1), :
                ]
        outs[turn][...] = packed[: (STEPS - turn) * MOVES].astype(BF16)


def pack_queries(me, moving, queries, fresh):
    width = queries.shape[2] + fresh.shape[2]
    return pl.pallas_call(
        pack_queries_kernel,
        out_shape=[
            jax.ShapeDtypeStruct(((STEPS - turn) * MOVES, width), BF16)
            for turn in range(STEPS)
        ],
        in_specs=[SMEM_SPEC] + [HBM_SPEC] * 3,
        out_specs=[VMEM_SPEC] * STEPS,
        scratch_shapes=[
            pltpu.SMEM(moving.shape, jnp.int32),
            pltpu.VMEM(queries.shape, BF16),
            pltpu.VMEM(fresh.shape, BF16),
            pltpu.VMEM((STEPS, SLOTS, width), F32),
            pltpu.VMEM((STEPS * MOVES, width), F32),
            pltpu.SemaphoreType.DMA((3,)),
        ],
        compiler_params=params(VMEM_MOST),
        cost_estimate=cost(),
        name="pack_queries",
    )(me, moving, queries, fresh)


def released_kernel(*refs):
    del refs


def released(blocks, after):
    return pl.pallas_call(
        released_kernel,
        out_shape=[jax.ShapeDtypeStruct(block.shape, block.dtype) for block in blocks],
        in_specs=[ANY_SPEC] * (len(blocks) + len(after)),
        out_specs=[ANY_SPEC] * len(blocks),
        input_output_aliases={i: i for i in range(len(blocks))},
        cost_estimate=cost(),
        name="released",
    )(*blocks, *after)


def pack_kernel(me_ref, moving_in, table_in, lengths_in, fresh_in, pool_in, *rest):
    (far, both), rest = rest[:2], rest[2:]
    moving, table, lengths, fresh, pool, rows, sems = rest
    loads = fetch(
        (
            (moving_in, moving),
            (table_in, table),
            (lengths_in, lengths),
            (fresh_in, fresh),
            *parts_of(pool_in, pool),
        ),
        sems,
    )
    me = me_ref[0]
    for load in loads[:4]:
        load.wait()
    for step in range(STEPS):
        rows[step] = fresh[step].astype(F32)
    for load in loads[4:]:
        load.wait()
    for turn, target, start in ((0, far, 0), (2, both, 0), (1, both, MOVES)):
        for m in range(MOVES):
            slot = moving[turn, m, me]
            for page in range(PAGES):
                target[(start + m) * PAGES + page] = pool[table[0, slot * PAGES + page]]
        for step in range(turn):
            items = []
            for m in range(MOVES):
                slot = moving[turn, m, me]
                position = lengths[me, slot] + step
                items.append(
                    (
                        (start + m) * PAGES + lax.shift_right_logical(position, 4),
                        rows[step, pl.ds(slot, 1), :],
                        position & (TOKENS - 1),
                    )
                )
            put_tokens(target, items)


def pack(me, moving, table, lengths, fresh, pool):
    return pl.pallas_call(
        pack_kernel,
        out_shape=[
            jax.ShapeDtypeStruct((size * PAGES,) + pool.shape[1:], BF16)
            for size in (MOVES, 2 * MOVES)
        ],
        in_specs=[SMEM_SPEC] + [HBM_SPEC] * 5,
        out_specs=[VMEM_SPEC] * 2,
        scratch_shapes=[
            pltpu.SMEM(moving.shape, jnp.int32),
            pltpu.SMEM(table.shape, jnp.int32),
            pltpu.SMEM(lengths.shape, jnp.int32),
            pltpu.VMEM(fresh.shape, BF16),
            pltpu.VMEM(pool.shape, BF16),
            pltpu.VMEM(fresh.shape, F32),
            pltpu.SemaphoreType.DMA((4 + CHUNKS,)),
        ],
        compiler_params=params(VMEM_MOST),
        cost_estimate=cost(),
        name="pack",
    )(me, moving, table, lengths, fresh, pool)


def gathered(pages, table, slot):
    return jnp.concatenate(
        [pages[table[0, slot * PAGES + page]] for page in range(PAGES)], axis=0
    )


def mark_slots(marks, moving, me):
    for slot in range(SLOTS):
        marks[slot] = STEPS
    for turn in range(STEPS):
        for m in range(MOVES):
            marks[moving[turn, m, me]] = turn


def serve_kernel(me_ref, moving, table, lengths, *rest):
    asked, rest = rest[:STEPS], rest[STEPS:]
    queries, fresh, far, both, pool, weight, out, cache, *rest = rest
    pages, taken, weights, products, query, result, rows, asker, answer, row_list, packed, marks, *sems = rest
    me = me_ref[0]
    block = MOVES * PAGES
    width = GROUP * HEAD
    parts, rows_out, column = products.shape
    moved_loads = fetch(
        (
            (far, taken.at[pl.ds(0, block)]),
            (both.at[pl.ds(block, block)], taken.at[pl.ds(block, block)]),
            (both.at[pl.ds(0, block)], taken.at[pl.ds(2 * block, block)]),
        ),
        sems[0],
    )
    pool_loads = fetch(parts_of(pool, pages), sems[1])
    weight_loads = fetch(
        [
            (weight.at[:, pl.ds(part * column, column)], weights.at[part])
            for part in range(parts)
        ],
        sems[2],
    )

    asker[...] = jnp.zeros_like(asker)
    counts = []
    for turn in range(STEPS):
        held = [lengths[me, moving[turn, m, me]] for m in range(MOVES)]
        counts += held
        moved_loads[turn].wait()
        for step in range(turn, STEPS):
            first = (step - turn) * MOVES
            row_list[...] = asked[turn][first : first + MOVES, :].astype(F32)
            for head in range(GROUP):
                asker[turn * MOVES : (turn + 1) * MOVES, step * GROUP + head, :] = row_list[
                    :, head * HEAD : (head + 1) * HEAD
                ]
            put_tokens(
                taken,
                [
                    (
                        turn * block + m * PAGES + lax.shift_right_logical(held[m] + step, 4),
                        row_list[m : m + 1, width:],
                        (held[m] + step) & (TOKENS - 1),
                    )
                    for m in range(MOVES)
                ],
            )
    values = attend_block(
        [
            taken[i * PAGES : (i + 1) * PAGES].reshape(PAGES * TOKENS, 2 * HEAD)
            for i in range(STEPS * MOVES)
        ],
        [asker[i].astype(BF16) for i in range(STEPS * MOVES)],
        counts,
    )
    for i, value in enumerate(values):
        answer[i] = value

    query[...] = jnp.zeros_like(query)
    for step in range(STEPS):
        rows[step] = fresh[step].astype(F32)
        for head in range(GROUP):
            query[:, step * GROUP + head, :] = queries[
                step, :, head * HEAD : (head + 1) * HEAD
            ].astype(F32)
    mark_slots(marks, moving, me)
    for load in pool_loads:
        load.wait()

    @pl.loop(0, SLOTS // MOVES)
    def _(group):
        slots = [group * MOVES + m for m in range(MOVES)]
        held = [lengths[me, slot] for slot in slots]
        for step in range(STEPS):
            items = []
            for slot, length in zip(slots, held):
                position = length + step
                page = table[0, slot * PAGES + lax.shift_right_logical(position, 4)]
                items.append(
                    (page, rows[step, pl.ds(slot, 1), :], position & (TOKENS - 1))
                )
            put_tokens(pages, items)

    stores = fetch(parts_of(pages, cache), sems[1])

    @pl.loop(0, SLOTS // BATCH)
    def _(group):
        slots = [group * BATCH + m for m in range(BATCH)]
        values = attend_block(
            [gathered(pages, table, slot) for slot in slots],
            [query[slot].astype(BF16) for slot in slots],
            [lengths[me, slot] for slot in slots],
        )
        for slot, value in zip(slots, values):
            result[slot] = value

    start = 0
    for step in range(STEPS):
        natural = jnp.concatenate(
            [result[:, step * GROUP + head, :] for head in range(GROUP)], axis=1
        )
        row = start
        for slot in range(SLOTS):
            packed[pl.ds(row, 1), :] = natural[slot : slot + 1, :]
            row = row + (marks[slot] > step).astype(jnp.int32)
        start += KEPT[step]
    for turn in range(STEPS):
        for step in range(turn, STEPS):
            packed[start : start + MOVES, :] = jnp.concatenate(
                [
                    answer[turn * MOVES : (turn + 1) * MOVES, step * GROUP + head, :]
                    for head in range(GROUP)
                ],
                axis=1,
            )
            start += MOVES
    whole = packed[:start].astype(BF16)
    copies = []
    for part, load in enumerate(weight_loads):
        load.wait()
        products[part] = jnp.dot(
            whole, weights[part], preferred_element_type=F32
        ).astype(BF16)
        copies += fetch([(products.at[part], out.at[part])], sems[3].at[pl.ds(part, 1)])
    for copy in copies + stores:
        copy.wait()


def serve(me, moving, table, lengths, asked, queries, fresh, far, both, pool, weight, parts):
    page = pool.shape[1:]
    count = STEPS * MOVES
    depth, features = weight.shape
    column = features // parts
    rows = sum(KEPT) + sum(MOVED)
    return pl.pallas_call(
        serve_kernel,
        out_shape=[
            jax.ShapeDtypeStruct((parts, rows, column), BF16),
            jax.ShapeDtypeStruct(pool.shape, BF16),
        ],
        in_specs=[SMEM_SPEC] * 4 + [VMEM_SPEC] * (STEPS + 2) + [ANY_SPEC] * 4,
        out_specs=[ANY_SPEC] * 2,
        scratch_shapes=[
            pltpu.VMEM(pool.shape, BF16),
            pltpu.VMEM((count * PAGES,) + page, BF16),
            pltpu.VMEM((parts, depth, column), BF16),
            pltpu.VMEM((parts, rows, column), BF16),
            pltpu.VMEM((SLOTS, ROWS, HEAD), F32),
            pltpu.VMEM((SLOTS, ROWS, HEAD), F32),
            pltpu.VMEM(fresh.shape, F32),
            pltpu.VMEM((count, ROWS, HEAD), F32),
            pltpu.VMEM((count, ROWS, HEAD), F32),
            pltpu.VMEM((MOVES, asked[0].shape[1]), F32),
            pltpu.VMEM((rows + 8, depth), F32),
            pltpu.SMEM((SLOTS,), jnp.int32),
            pltpu.SemaphoreType.DMA((STEPS,)),
            pltpu.SemaphoreType.DMA((CHUNKS,)),
            pltpu.SemaphoreType.DMA((parts,)),
            pltpu.SemaphoreType.DMA((parts,)),
        ],
        compiler_params=params(VMEM_MOST),
        cost_estimate=cost(),
        name="serve",
    )(me, moving, table, lengths, *asked, queries, fresh, far, both, pool, weight)


def store_pages_kernel(turns, pieces, hops, me_ref, moving, table, lengths, fresh, *rest):
    arrived, (_, cache, note, pages, rows, sem) = rest[: len(pieces)], rest[len(pieces) :]
    note[...] = jnp.zeros_like(note)
    me = me_ref[0]
    block = MOVES * PAGES
    instances = lengths.shape[0]
    for step in range(min(turns), STEPS):
        rows[step] = fresh[step].astype(F32)
    for (start, size), piece in zip(pieces, arrived):
        pages[start : start + size] = piece[:size]
    for i, turn in enumerate(turns):
        source = lax.rem(me - hops[turn] + instances, instances)
        slots = [moving[turn, m, me] for m in range(MOVES)]
        held = [lengths[source, moving[turn, m, source]] for m in range(MOVES)]
        for step in range(turn, STEPS):
            put_tokens(
                pages,
                [
                    (
                        i * block + m * PAGES + lax.shift_right_logical(held[m] + step, 4),
                        rows[step, pl.ds(slots[m], 1), :],
                        (held[m] + step) & (TOKENS - 1),
                    )
                    for m in range(MOVES)
                ],
            )
        for m in range(MOVES):
            for page in range(PAGES):
                pltpu.make_async_copy(
                    pages.at[i * block + m * PAGES + page],
                    cache.at[table[0, slots[m] * PAGES + page]],
                    sem,
                ).start()
    pltpu.make_async_copy(pages, cache.at[pl.ds(0, len(turns) * block)], sem).wait()


def store_pages(turns, pieces, hops, me, moving, table, lengths, fresh, arrived, cache):
    return pl.pallas_call(
        functools.partial(store_pages_kernel, turns, pieces, hops),
        out_shape=[
            jax.ShapeDtypeStruct(cache.shape, BF16),
            jax.ShapeDtypeStruct((8, HEAD), F32),
        ],
        in_specs=[SMEM_SPEC] * 4 + [VMEM_SPEC] * (1 + len(arrived)) + [ANY_SPEC],
        out_specs=[ANY_SPEC, VMEM_SPEC],
        scratch_shapes=[
            pltpu.VMEM((len(turns) * MOVES * PAGES,) + cache.shape[1:], BF16),
            pltpu.VMEM(fresh.shape, F32),
            pltpu.SemaphoreType.DMA,
        ],
        input_output_aliases={5 + len(arrived): 0},
        compiler_params=params(),
        cost_estimate=cost(),
        name="store_pages",
    )(me, moving, table, lengths, fresh, *arrived, cache)


def settle_kernel(me_ref, moving, partial, _, natural, *rest):
    outs, (kept, marks) = rest[:STEPS], rest[STEPS:]
    mark_slots(marks, moving, me_ref[0])
    total = partial[0].astype(F32)
    for part in range(1, partial.shape[0]):
        total = total + partial[part].astype(F32)
    kept[...] = total
    row = 0
    for step in range(STEPS):
        index = row
        for slot in range(SLOTS):
            natural[step * SLOTS + slot : step * SLOTS + slot + 1, :] = kept[
                pl.ds(index, 1), :
            ]
            index = index + (marks[slot] > step).astype(jnp.int32)
        row += KEPT[step]
    for turn, out in enumerate(outs):
        out[...] = kept[row : row + MOVED[turn]].astype(BF16)
        row += MOVED[turn]


def settle(me, moving, partial, after):
    _, rows, column = partial.shape
    out = pl.pallas_call(
        settle_kernel,
        out_shape=[jax.ShapeDtypeStruct((STEPS * SLOTS, column), F32)]
        + [jax.ShapeDtypeStruct((count, column), BF16) for count in MOVED],
        in_specs=[SMEM_SPEC] * 2 + [VMEM_SPEC] * 2,
        out_specs=[VMEM_SPEC] * (1 + STEPS),
        scratch_shapes=[
            pltpu.VMEM((rows, column), F32),
            pltpu.SMEM((SLOTS,), jnp.int32),
        ],
        compiler_params=params(),
        cost_estimate=cost(),
        name="settle",
    )(me, moving, partial, after)
    return out[0], out[1:]


def assemble_kernel(me_ref, moving, natural, *rest):
    taken, (_, out, rows) = rest[:STEPS], rest[STEPS:]
    me = me_ref[0]
    rows[...] = natural[...]
    for turn, block in enumerate(taken):
        values = block[...].astype(F32)
        for step in range(turn, STEPS):
            for m in range(MOVES):
                k = (step - turn) * MOVES + m
                rows[pl.ds(step * SLOTS + moving[turn, m, me], 1), :] = values[k : k + 1, :]
    out[...] = rows[...].astype(BF16)


def assemble(me, moving, natural, taken, after):
    return pl.pallas_call(
        assemble_kernel,
        out_shape=jax.ShapeDtypeStruct(natural.shape, BF16),
        in_specs=[SMEM_SPEC] * 2 + [VMEM_SPEC] * (2 + STEPS),
        out_specs=VMEM_SPEC,
        scratch_shapes=[pltpu.VMEM(natural.shape, F32)],
        compiler_params=params(),
        cost_estimate=cost(),
        name="assemble",
    )(me, moving, natural, *taken, after)


def shards(queries, incoming, pool, table, lengths, moving, weight):
    count = lax.axis_size("inst")
    parts = lax.axis_size("tp")
    me = lax.axis_index("inst").reshape(1)
    hops = tuple(count // 2 ** (step + 1) for step in range(STEPS))
    fresh = incoming.reshape(STEPS, SLOTS, 2 * HEAD)
    own = pool.reshape(pool.shape[0], TOKENS, 2 * HEAD)

    moving = moving.transpose(0, 2, 1)
    block = MOVES * PAGES
    asked = pack_queries(me, moving, queries, fresh)
    asked = [shifted(rows, -hop) for rows, hop in zip(asked, hops)]
    far, both = pack(me, moving, table, lengths, fresh, own)
    far, both = released((far, both), asked)
    far_one = shifted(far, -hops[1])
    both_in = shifted(both, hops[2])
    partial, cache = serve(
        me, moving, table, lengths, asked, queries, fresh, far, both, own, weight, parts
    )
    partial = lax.all_to_all(partial, "tp", 0, 0, tiled=True)
    mid_in = shifted(both_in[block:], hops[1] - hops[2])
    far_two = shifted(far_one, -hops[2])
    far_in = shifted(far_two, -hops[2])

    common = (hops, me, moving, table, lengths, fresh)
    cache, stored = store_pages(
        (1, 2), ((0, block), (block, block)), *common, (mid_in, both_in), cache
    )
    natural, back = settle(me, moving, partial, stored)
    back = [shifted(rows, hop) for rows, hop in zip(back, hops)]
    cache, stored = store_pages((0,), ((0, block),), *common, (far_in,), cache)
    attended = assemble(me, moving, natural, back, stored)
    return attended.reshape(queries.shape), cache.reshape(pool.shape)


def solution(mesh):
    placed = (
        P(None, "inst", "tp"),
        P(None, "inst", "tp", None),
        P("inst", "tp", None, None),
        P("inst", None),
        P(),
        P(),
        P("tp", None),
    )
    return jax.shard_map(
        shards,
        mesh=mesh,
        in_specs=placed,
        out_specs=(P(None, "inst", "tp"), P("inst", "tp", None, None)),
        check_vma=False,
    )
```

```python
import functools

import jax
import jax.numpy as jnp
from jax import lax
from jax.experimental import pallas as pl
from jax.experimental.pallas import tpu as pltpu
from jax.sharding import PartitionSpec as P

F32 = jnp.float32
BF16 = jnp.bfloat16
STEPS = 3
SLOTS = 64
PAGES = 8
TOKENS = 16
MOVES = 8
HEAD = 128
GROUP = 4
ROWS = 16
CHUNKS = 8
KEPT = tuple(SLOTS - MOVES * (step + 1) for step in range(STEPS))
MOVED = tuple(MOVES * (STEPS - turn) for turn in range(STEPS))
BATCH = 32
FAR = 60
LEAD = 3
VMEM_MOST = 63 * 1024 * 1024
VMEM_MORE = 61 * 1024 * 1024
VMEM_SOME = 20 * 1024 * 1024

SMEM_SPEC = pl.BlockSpec(memory_space=pltpu.SMEM)
VMEM_SPEC = pl.BlockSpec(memory_space=pltpu.VMEM)
ANY_SPEC = pl.BlockSpec(memory_space=pl.ANY)
HBM_SPEC = pl.BlockSpec(memory_space=pltpu.HBM)


def params(limit=VMEM_SOME):
    return pltpu.CompilerParams(vmem_limit_bytes=limit)


def cost():
    return pl.CostEstimate(flops=1, bytes_accessed=1, transcendentals=0)


def fetch(pairs, sems):
    copies = [
        pltpu.make_async_copy(source, target, sems.at[k])
        for k, (source, target) in enumerate(pairs)
    ]
    for copy in copies:
        copy.start()
    return copies


def shifted(block, distance):
    count = lax.axis_size("inst")
    return lax.ppermute(
        block, "inst", [((i - distance) % count, i) for i in range(count)]
    )


def with_token(page, token, offset):
    row = lax.broadcasted_iota(jnp.int32, page.shape, 0)
    return jnp.where(row == offset, token.astype(F32), page.astype(F32)).astype(BF16)


def put_tokens(pages, items):
    changed = [with_token(pages[page], token, offset) for page, token, offset in items]
    for (page, _, _), value in zip(items, changed):
        pages[page] = value


def parts_of(source, target):
    size = source.shape[0] // CHUNKS
    return [
        (source.at[pl.ds(k * size, size)], target.at[pl.ds(k * size, size)])
        for k in range(CHUNKS)
    ]


def attend_block(pages, queries, counts):
    scores = jnp.concatenate(
        [
            lax.dot_general(
                query,
                page[:, :HEAD],
                (((1,), (1,)), ((), ())),
                preferred_element_type=F32,
            )
            for page, query in zip(pages, queries)
        ],
        axis=0,
    ) * (HEAD**-0.5)
    lane = lax.broadcasted_iota(jnp.int32, (ROWS, HEAD), 1)
    step = lax.shift_right_logical(lax.broadcasted_iota(jnp.int32, (ROWS, HEAD), 0), 2)
    lag = lane - step
    live = jnp.concatenate([lag - count for count in counts], axis=0) <= 0
    scores = jnp.where(live, scores, -jnp.inf)
    exp_part = jnp.exp(scores - jnp.max(scores, axis=1, keepdims=True))
    weights = exp_part * (1.0 / jnp.sum(exp_part, axis=1, keepdims=True))
    weights = weights.astype(BF16)
    return [
        jnp.dot(
            weights[i * ROWS : (i + 1) * ROWS],
            page[:, HEAD:],
            preferred_element_type=F32,
        )
        for i, page in enumerate(pages)
    ]


def pack_queries_kernel(moving_in, queries_in, fresh_in, *rest):
    outs, (moving, queries, fresh, natural, packed, sems) = rest[:STEPS], rest[STEPS:]
    loads = fetch(
        ((moving_in, moving), (queries_in, queries), (fresh_in, fresh)), sems
    )
    me = lax.axis_index("inst")
    width = GROUP * HEAD
    for load in loads:
        load.wait()
    for step in range(STEPS):
        natural[step, :, :width] = queries[step].astype(F32)
        natural[step, :, width:] = fresh[step].astype(F32)
    for turn in range(STEPS):
        for m in range(MOVES):
            slot = moving[turn, m, me]
            for step in range(turn, STEPS):
                packed[pl.ds((step - turn) * MOVES + m, 1), :] = natural[
                    step, pl.ds(slot, 1), :
                ]
        outs[turn][...] = packed[: (STEPS - turn) * MOVES].astype(BF16)


def pack_queries(moving, queries, fresh):
    width = queries.shape[2] + fresh.shape[2]
    return pl.pallas_call(
        pack_queries_kernel,
        out_shape=[
            jax.ShapeDtypeStruct(((STEPS - turn) * MOVES, width), BF16)
            for turn in range(STEPS)
        ],
        in_specs=[HBM_SPEC] * 3,
        out_specs=[VMEM_SPEC] * STEPS,
        scratch_shapes=[
            pltpu.SMEM(moving.shape, jnp.int32),
            pltpu.VMEM(queries.shape, BF16),
            pltpu.VMEM(fresh.shape, BF16),
            pltpu.VMEM((STEPS, SLOTS, width), F32),
            pltpu.VMEM((STEPS * MOVES, width), F32),
            pltpu.SemaphoreType.DMA((3,)),
        ],
        compiler_params=params(VMEM_MOST),
        cost_estimate=cost(),
        name="pack_queries",
    )(moving, queries, fresh)


def released_kernel(*refs):
    del refs


def released(blocks, after):
    return pl.pallas_call(
        released_kernel,
        out_shape=[jax.ShapeDtypeStruct(block.shape, block.dtype) for block in blocks],
        in_specs=[ANY_SPEC] * (len(blocks) + len(after)),
        out_specs=[ANY_SPEC] * len(blocks),
        input_output_aliases={i: i for i in range(len(blocks))},
        cost_estimate=cost(),
        name="released",
    )(*blocks, *after)


def pack_kernel(moving_in, table_in, lengths_in, fresh_in, pool_in, *rest):
    (far, direct, both), rest = rest[:3], rest[3:]
    moving, table, lengths, fresh, pool, rows, sems = rest
    loads = fetch(
        (
            (moving_in, moving),
            (table_in, table),
            (lengths_in, lengths),
            (fresh_in, fresh),
            *parts_of(pool_in, pool),
        ),
        sems,
    )
    me = lax.axis_index("inst")
    for load in loads[:4]:
        load.wait()
    for step in range(STEPS):
        rows[step] = fresh[step].astype(F32)
    for load in loads[4:]:
        load.wait()
    for turn, target, start in ((0, far, 0), (2, both, 0), (1, both, MOVES)):
        for m in range(MOVES):
            slot = moving[turn, m, me]
            for page in range(PAGES):
                target[(start + m) * PAGES + page] = pool[table[0, slot * PAGES + page]]
        if turn == 0:
            direct[...] = far[FAR :]
        for step in range(turn):
            items = []
            for m in range(MOVES):
                slot = moving[turn, m, me]
                position = lengths[me, slot] + step
                items.append(
                    (
                        (start + m) * PAGES + lax.shift_right_logical(position, 4),
                        rows[step, pl.ds(slot, 1), :],
                        position & (TOKENS - 1),
                    )
                )
            put_tokens(target, items)


def pack(moving, table, lengths, fresh, pool):
    return pl.pallas_call(
        pack_kernel,
        out_shape=[
            jax.ShapeDtypeStruct((size,) + pool.shape[1:], BF16)
            for size in (MOVES * PAGES, MOVES * PAGES - FAR, 2 * MOVES * PAGES)
        ],
        in_specs=[HBM_SPEC] * 5,
        out_specs=[VMEM_SPEC] * 3,
        scratch_shapes=[
            pltpu.SMEM(moving.shape, jnp.int32),
            pltpu.SMEM(table.shape, jnp.int32),
            pltpu.SMEM(lengths.shape, jnp.int32),
            pltpu.VMEM(fresh.shape, BF16),
            pltpu.VMEM(pool.shape, BF16),
            pltpu.VMEM(fresh.shape, F32),
            pltpu.SemaphoreType.DMA((4 + CHUNKS,)),
        ],
        compiler_params=params(VMEM_MOST),
        cost_estimate=cost(),
        name="pack",
    )(moving, table, lengths, fresh, pool)


def gathered(pages, table, slot):
    return jnp.concatenate(
        [pages[table[0, slot * PAGES + page]] for page in range(PAGES)], axis=0
    )


def mark_slots(marks, moving, me):
    for slot in range(SLOTS):
        marks[slot] = STEPS
    for turn in range(STEPS):
        for m in range(MOVES):
            marks[moving[turn, m, me]] = turn


def serve_kernel(moving_in, table_in, lengths_in, *rest):
    asked_in, rest = rest[:STEPS], rest[STEPS:]
    queries_in, fresh_in, far, both, pool, weight, out, cache, *rest = rest
    moving, table, lengths, queries, fresh, *rest = rest
    asked, rest = rest[:STEPS], rest[STEPS:]
    pages, taken, weights, products, query, result, rows, asker, answer, row_list, packed, marks, *sems = rest
    me = lax.axis_index("inst")
    block = MOVES * PAGES
    width = GROUP * HEAD
    parts, rows_out, column = products.shape
    small_loads = fetch(
        (
            (moving_in, moving),
            (lengths_in, lengths),
            *zip(asked_in, asked),
            (table_in, table),
            (queries_in, queries),
            (fresh_in, fresh),
        ),
        sems[4],
    )
    moved_loads = fetch(
        (
            (far, taken.at[pl.ds(0, block)]),
            (both.at[pl.ds(block, block)], taken.at[pl.ds(block, block)]),
            (both.at[pl.ds(0, block)], taken.at[pl.ds(2 * block, block)]),
        ),
        sems[0],
    )
    pool_loads = fetch(parts_of(pool, pages), sems[1])
    weight_loads = fetch(
        [
            (weight.at[:, pl.ds(part * column, column)], weights.at[part])
            for part in range(parts)
        ],
        sems[2],
    )

    asker[...] = jnp.zeros_like(asker)
    query[...] = jnp.zeros_like(query)
    for load in small_loads:
        load.wait()
    counts = []
    for turn in range(STEPS):
        held = [lengths[me, moving[turn, m, me]] for m in range(MOVES)]
        counts += held
        moved_loads[turn].wait()
        for step in range(turn, STEPS):
            first = (step - turn) * MOVES
            row_list[...] = asked[turn][first : first + MOVES, :].astype(F32)
            for head in range(GROUP):
                asker[turn * MOVES : (turn + 1) * MOVES, step * GROUP + head, :] = row_list[
                    :, head * HEAD : (head + 1) * HEAD
                ]
            put_tokens(
                taken,
                [
                    (
                        turn * block + m * PAGES + lax.shift_right_logical(held[m] + step, 4),
                        row_list[m : m + 1, width:],
                        (held[m] + step) & (TOKENS - 1),
                    )
                    for m in range(MOVES)
                ],
            )
    values = attend_block(
        [
            taken[i * PAGES : (i + 1) * PAGES].reshape(PAGES * TOKENS, 2 * HEAD)
            for i in range(STEPS * MOVES)
        ],
        [asker[i].astype(BF16) for i in range(STEPS * MOVES)],
        counts,
    )
    for i, value in enumerate(values):
        answer[i] = value

    for step in range(STEPS):
        rows[step] = fresh[step].astype(F32)
        for head in range(GROUP):
            query[:, step * GROUP + head, :] = queries[
                step, :, head * HEAD : (head + 1) * HEAD
            ].astype(F32)
    mark_slots(marks, moving, me)
    for load in pool_loads:
        load.wait()

    @pl.loop(0, SLOTS // MOVES)
    def _(group):
        slots = [group * MOVES + m for m in range(MOVES)]
        held = [lengths[me, slot] for slot in slots]
        for step in range(STEPS):
            items = []
            for slot, length in zip(slots, held):
                position = length + step
                page = table[0, slot * PAGES + lax.shift_right_logical(position, 4)]
                items.append(
                    (page, rows[step, pl.ds(slot, 1), :], position & (TOKENS - 1))
                )
            put_tokens(pages, items)

    stores = fetch(parts_of(pages, cache), sems[1])

    @pl.loop(0, SLOTS // BATCH)
    def _(group):
        slots = [group * BATCH + m for m in range(BATCH)]
        values = attend_block(
            [gathered(pages, table, slot) for slot in slots],
            [query[slot].astype(BF16) for slot in slots],
            [lengths[me, slot] for slot in slots],
        )
        for slot, value in zip(slots, values):
            result[slot] = value

    start = 0
    for step in range(STEPS):
        natural = jnp.concatenate(
            [result[:, step * GROUP + head, :] for head in range(GROUP)], axis=1
        )
        row = start
        for slot in range(SLOTS):
            packed[pl.ds(row, 1), :] = natural[slot : slot + 1, :]
            row = row + (marks[slot] > step).astype(jnp.int32)
        start += KEPT[step]
    for turn in range(STEPS):
        for step in range(turn, STEPS):
            packed[start : start + MOVES, :] = jnp.concatenate(
                [
                    answer[turn * MOVES : (turn + 1) * MOVES, step * GROUP + head, :]
                    for head in range(GROUP)
                ],
                axis=1,
            )
            start += MOVES
    whole = packed[:start].astype(BF16)
    copies = []
    for part, load in enumerate(weight_loads):
        load.wait()
        products[part] = jnp.dot(
            whole, weights[part], preferred_element_type=F32
        ).astype(BF16)
        copies += fetch([(products.at[part], out.at[part])], sems[3].at[pl.ds(part, 1)])
    for copy in copies + stores:
        copy.wait()


def serve(moving, table, lengths, asked, queries, fresh, far, both, pool, weight, parts):
    page = pool.shape[1:]
    count = STEPS * MOVES
    kept_rows = sum(KEPT)
    depth, features = weight.shape
    column = features // parts
    total = kept_rows + sum(MOVED)
    return pl.pallas_call(
        serve_kernel,
        out_shape=[
            jax.ShapeDtypeStruct((parts, total, column), BF16),
            jax.ShapeDtypeStruct(pool.shape, BF16),
        ],
        in_specs=[ANY_SPEC] * (STEPS + 9),
        out_specs=[ANY_SPEC] * 2,
        scratch_shapes=[
            pltpu.SMEM(moving.shape, jnp.int32),
            pltpu.SMEM(table.shape, jnp.int32),
            pltpu.SMEM(lengths.shape, jnp.int32),
            pltpu.VMEM(queries.shape, BF16),
            pltpu.VMEM(fresh.shape, BF16),
            *[pltpu.VMEM(rows.shape, BF16) for rows in asked],
            pltpu.VMEM(pool.shape, BF16),
            pltpu.VMEM((count * PAGES,) + page, BF16),
            pltpu.VMEM((parts, depth, column), BF16),
            pltpu.VMEM((parts, total, column), BF16),
            pltpu.VMEM((SLOTS, ROWS, HEAD), F32),
            pltpu.VMEM((SLOTS, ROWS, HEAD), F32),
            pltpu.VMEM(fresh.shape, F32),
            pltpu.VMEM((count, ROWS, HEAD), F32),
            pltpu.VMEM((count, ROWS, HEAD), F32),
            pltpu.VMEM((MOVES, asked[0].shape[1]), F32),
            pltpu.VMEM((total + 8, depth), F32),
            pltpu.SMEM((SLOTS,), jnp.int32),
            pltpu.SemaphoreType.DMA((STEPS,)),
            pltpu.SemaphoreType.DMA((CHUNKS,)),
            pltpu.SemaphoreType.DMA((parts,)),
            pltpu.SemaphoreType.DMA((parts,)),
            pltpu.SemaphoreType.DMA((STEPS + 5,)),
        ],
        compiler_params=params(VMEM_MORE),
        cost_estimate=cost(),
        name="serve",
    )(moving, table, lengths, *asked, queries, fresh, far, both, pool, weight)


def insert_and_store(turn, hop, moving, table, lengths, rows, pages, cache, sem):
    me = lax.axis_index("inst")
    instances = lengths.shape[0]
    source = lax.rem(me - hop + instances, instances)
    slots = [moving[turn, m, me] for m in range(MOVES)]
    held = [lengths[source, moving[turn, m, source]] for m in range(MOVES)]
    for step in range(turn, STEPS):
        put_tokens(
            pages,
            [
                (
                    m * PAGES + lax.shift_right_logical(held[m] + step, 4),
                    rows[step, pl.ds(slots[m], 1), :],
                    (held[m] + step) & (TOKENS - 1),
                )
                for m in range(MOVES)
            ],
        )
    for m in range(MOVES):
        for page in range(PAGES):
            pltpu.make_async_copy(
                pages.at[m * PAGES + page],
                cache.at[table[0, slots[m] * PAGES + page]],
                sem,
            ).start()


def store_pages_kernel(turn, hop, moving, table, lengths, fresh, arrived, *rest):
    _, cache, *surplus, pages, rows, sem = rest
    for step in range(turn, STEPS):
        rows[step] = fresh[step].astype(F32)
    pages[...] = arrived[: MOVES * PAGES]
    insert_and_store(turn, hop, moving, table, lengths, rows, pages, cache, sem)
    for left in surplus:
        left[...] = arrived[MOVES * PAGES :]
    pltpu.make_async_copy(pages, cache.at[pl.ds(0, MOVES * PAGES)], sem).wait()


def store_pages(turn, hop, moving, table, lengths, fresh, arrived, cache):
    surplus = arrived.shape[0] - MOVES * PAGES
    return pl.pallas_call(
        functools.partial(store_pages_kernel, turn, hop),
        out_shape=[jax.ShapeDtypeStruct(cache.shape, BF16)]
        + [jax.ShapeDtypeStruct((surplus,) + cache.shape[1:], BF16)] * (surplus > 0),
        in_specs=[SMEM_SPEC] * 3 + [VMEM_SPEC] * 2 + [ANY_SPEC],
        out_specs=[ANY_SPEC] + [VMEM_SPEC] * (surplus > 0),
        scratch_shapes=[
            pltpu.VMEM((MOVES * PAGES,) + cache.shape[1:], BF16),
            pltpu.VMEM(fresh.shape, F32),
            pltpu.SemaphoreType.DMA,
        ],
        input_output_aliases={5: 0},
        compiler_params=params(),
        cost_estimate=cost(),
        name="store_pages",
    )(moving, table, lengths, fresh, arrived, cache)


def settle_kernel(moving, partial, direct, natural, *rest):
    outs, (kept, marks) = rest[:STEPS], rest[STEPS:]
    mark_slots(marks, moving, lax.axis_index("inst"))
    total = partial[0].astype(F32)
    for part in range(1, partial.shape[0]):
        total = total + partial[part].astype(F32)
    kept[...] = total
    row = 0
    for step in range(STEPS):
        index = row
        for slot in range(SLOTS):
            natural[step * SLOTS + slot : step * SLOTS + slot + 1, :] = kept[
                pl.ds(index, 1), :
            ]
            index = index + (marks[slot] > step).astype(jnp.int32)
        row += KEPT[step]
    for turn, out in enumerate(outs):
        value = kept[row : row + MOVED[turn]]
        row += MOVED[turn]
        if turn == 0:
            flat = jnp.concatenate([value[:, : 2 * HEAD], value[:, 2 * HEAD :]], axis=0)
            out[:LEAD] = flat.reshape(LEAD, TOKENS, 2 * HEAD).astype(BF16)
            out[LEAD:] = direct[...]
        else:
            out[...] = value.astype(BF16)


def settle(moving, partial, direct):
    _, rows, column = partial.shape
    out = pl.pallas_call(
        settle_kernel,
        out_shape=[jax.ShapeDtypeStruct((STEPS * SLOTS, column), F32)]
        + [jax.ShapeDtypeStruct((LEAD + direct.shape[0],) + direct.shape[1:], BF16)]
        + [jax.ShapeDtypeStruct((count, column), BF16) for count in MOVED[1:]],
        in_specs=[SMEM_SPEC] + [VMEM_SPEC] * 2,
        out_specs=[VMEM_SPEC] * (1 + STEPS),
        scratch_shapes=[
            pltpu.VMEM((rows, column), F32),
            pltpu.SMEM((SLOTS,), jnp.int32),
        ],
        compiler_params=params(),
        cost_estimate=cost(),
        name="settle",
    )(moving, partial, direct)
    return out[0], out[1:]


def finish_kernel(hop, moving, table, lengths, fresh, far, natural, *rest):
    taken, (_, out, cache, pages, rows, total, sem) = rest[:STEPS], rest[STEPS:]
    for step in range(STEPS):
        rows[step] = fresh[step].astype(F32)
    pages[: far.shape[0]] = far[...]
    pages[far.shape[0] :] = taken[0][LEAD:]
    insert_and_store(0, hop, moving, table, lengths, rows, pages, cache, sem)
    me = lax.axis_index("inst")
    total[...] = natural[...]
    for turn, block in enumerate(taken):
        if turn == 0:
            flat = block[:LEAD].astype(F32).reshape(LEAD * TOKENS, 2 * HEAD)
            values = jnp.concatenate([flat[: MOVED[0]], flat[MOVED[0] :]], axis=1)
        else:
            values = block[...].astype(F32)
        for step in range(turn, STEPS):
            for m in range(MOVES):
                k = (step - turn) * MOVES + m
                total[pl.ds(step * SLOTS + moving[turn, m, me], 1), :] = values[k : k + 1, :]
    out[...] = total[...].astype(BF16)
    pltpu.make_async_copy(pages, cache.at[pl.ds(0, MOVES * PAGES)], sem).wait()


def finish(hop, moving, table, lengths, fresh, far, natural, taken, cache):
    return pl.pallas_call(
        functools.partial(finish_kernel, hop),
        out_shape=[
            jax.ShapeDtypeStruct(natural.shape, BF16),
            jax.ShapeDtypeStruct(cache.shape, BF16),
        ],
        in_specs=[SMEM_SPEC] * 3 + [VMEM_SPEC] * (3 + STEPS) + [ANY_SPEC],
        out_specs=[VMEM_SPEC, ANY_SPEC],
        scratch_shapes=[
            pltpu.VMEM((MOVES * PAGES,) + cache.shape[1:], BF16),
            pltpu.VMEM(fresh.shape, F32),
            pltpu.VMEM(natural.shape, F32),
            pltpu.SemaphoreType.DMA,
        ],
        input_output_aliases={6 + STEPS: 1},
        compiler_params=params(),
        cost_estimate=cost(),
        name="finish",
    )(moving, table, lengths, fresh, far, natural, *taken, cache)


def shards(queries, incoming, pool, table, lengths, moving, weight):
    count = lax.axis_size("inst")
    parts = lax.axis_size("tp")
    hops = tuple(count // 2 ** (step + 1) for step in range(STEPS))
    fresh = incoming.reshape(STEPS, SLOTS, 2 * HEAD)
    own = pool.reshape(pool.shape[0], TOKENS, 2 * HEAD)

    moving = moving.transpose(0, 2, 1)
    block = MOVES * PAGES
    asked = pack_queries(moving, queries, fresh)
    asked = [shifted(rows, -hop) for rows, hop in zip(asked, hops)]
    far, direct, both = pack(moving, table, lengths, fresh, own)
    far, both = released((far, both), asked)
    both_in = shifted(both, hops[2])
    far_one = shifted(far, -hops[1])
    partial, cache = serve(
        moving, table, lengths, asked, queries, fresh, far, both, own, weight, parts
    )
    partial = lax.all_to_all(partial, "tp", 0, 0, tiled=True)
    common = (moving, table, lengths, fresh)
    cache, mid = store_pages(2, hops[2], *common, both_in, cache)
    mid_in = shifted(mid, hops[1] - hops[2])
    far_two = shifted(far_one[:FAR], -hops[2])
    far_in = shifted(far_two, -hops[2])
    natural, back = settle(moving, partial, direct)
    back = [shifted(rows, hop) for rows, hop in zip(back, hops)]
    (cache,) = store_pages(1, hops[1], *common, mid_in, cache)
    attended, cache = finish(hops[0], *common, far_in, natural, back, cache)
    return attended.reshape(queries.shape), cache.reshape(pool.shape)


def solution(mesh):
    placed = (
        P(None, "inst", "tp"),
        P(None, "inst", "tp", None),
        P("inst", "tp", None, None),
        P("inst", None),
        P(),
        P(),
        P("tp", None),
    )
    return jax.shard_map(
        shards,
        mesh=mesh,
        in_specs=placed,
        out_specs=(P(None, "inst", "tp"), P("inst", "tp", None, None)),
        check_vma=False,
    )
```

```python
import functools

import jax
import jax.numpy as jnp
from jax import lax
from jax.experimental import pallas as pl
from jax.experimental.pallas import tpu as pltpu
from jax.sharding import PartitionSpec as P

F32 = jnp.float32
BF16 = jnp.bfloat16
STEPS = 3
SLOTS = 64
PAGES = 8
TOKENS = 16
MOVES = 8
HEAD = 128
GROUP = 4
ROWS = 16
CHUNKS = 8
KEPT = tuple(SLOTS - MOVES * (step + 1) for step in range(STEPS))
MOVED = tuple(MOVES * (STEPS - turn) for turn in range(STEPS))
BATCH = 32
FAR = 58
LEAD = 3
VMEM_MOST = 63 * 1024 * 1024
VMEM_MORE = 61 * 1024 * 1024
VMEM_SOME = 20 * 1024 * 1024

SMEM_SPEC = pl.BlockSpec(memory_space=pltpu.SMEM)
VMEM_SPEC = pl.BlockSpec(memory_space=pltpu.VMEM)
ANY_SPEC = pl.BlockSpec(memory_space=pl.ANY)
HBM_SPEC = pl.BlockSpec(memory_space=pltpu.HBM)


def params(limit=VMEM_SOME):
    return pltpu.CompilerParams(vmem_limit_bytes=limit)


def cost():
    return pl.CostEstimate(flops=1, bytes_accessed=1, transcendentals=0)


def fetch(pairs, sems):
    copies = [
        pltpu.make_async_copy(source, target, sems.at[k])
        for k, (source, target) in enumerate(pairs)
    ]
    for copy in copies:
        copy.start()
    return copies


def shifted(block, distance):
    count = lax.axis_size("inst")
    return lax.ppermute(
        block, "inst", [((i - distance) % count, i) for i in range(count)]
    )


def with_token(page, token, offset):
    row = lax.broadcasted_iota(jnp.int32, page.shape, 0)
    return jnp.where(row == offset, token.astype(F32), page.astype(F32)).astype(BF16)


def put_tokens(pages, items):
    changed = [with_token(pages[page], token, offset) for page, token, offset in items]
    for (page, _, _), value in zip(items, changed):
        pages[page] = value


def parts_of(source, target):
    size = source.shape[0] // CHUNKS
    return [
        (source.at[pl.ds(k * size, size)], target.at[pl.ds(k * size, size)])
        for k in range(CHUNKS)
    ]


def attend_block(pages, queries, counts):
    scores = jnp.concatenate(
        [
            lax.dot_general(
                query,
                page[:, :HEAD],
                (((1,), (1,)), ((), ())),
                preferred_element_type=F32,
            )
            for page, query in zip(pages, queries)
        ],
        axis=0,
    ) * (HEAD**-0.5)
    lane = lax.broadcasted_iota(jnp.int32, (ROWS, HEAD), 1)
    step = lax.shift_right_logical(lax.broadcasted_iota(jnp.int32, (ROWS, HEAD), 0), 2)
    lag = lane - step
    live = jnp.concatenate([lag - count for count in counts], axis=0) <= 0
    scores = jnp.where(live, scores, -jnp.inf)
    exp_part = jnp.exp(scores - jnp.max(scores, axis=1, keepdims=True))
    weights = exp_part * (1.0 / jnp.sum(exp_part, axis=1, keepdims=True))
    weights = weights.astype(BF16)
    return [
        jnp.dot(
            weights[i * ROWS : (i + 1) * ROWS],
            page[:, HEAD:],
            preferred_element_type=F32,
        )
        for i, page in enumerate(pages)
    ]


def pack_queries_kernel(moving_in, queries_in, fresh_in, *rest):
    outs, (moving, queries, fresh, natural, packed, sems) = rest[:STEPS], rest[STEPS:]
    loads = fetch(
        ((moving_in, moving), (queries_in, queries), (fresh_in, fresh)), sems
    )
    me = lax.axis_index("inst")
    width = GROUP * HEAD
    for load in loads:
        load.wait()
    for step in range(STEPS):
        natural[step, :, :width] = queries[step].astype(F32)
        natural[step, :, width:] = fresh[step].astype(F32)
    for turn in range(STEPS):
        for m in range(MOVES):
            slot = moving[turn, m, me]
            for step in range(turn, STEPS):
                packed[pl.ds((step - turn) * MOVES + m, 1), :] = natural[
                    step, pl.ds(slot, 1), :
                ]
        outs[turn][...] = packed[: (STEPS - turn) * MOVES].astype(BF16)


def pack_queries(moving, queries, fresh):
    width = queries.shape[2] + fresh.shape[2]
    return pl.pallas_call(
        pack_queries_kernel,
        out_shape=[
            jax.ShapeDtypeStruct(((STEPS - turn) * MOVES, width), BF16)
            for turn in range(STEPS)
        ],
        in_specs=[HBM_SPEC] * 3,
        out_specs=[VMEM_SPEC] * STEPS,
        scratch_shapes=[
            pltpu.SMEM(moving.shape, jnp.int32),
            pltpu.VMEM(queries.shape, BF16),
            pltpu.VMEM(fresh.shape, BF16),
            pltpu.VMEM((STEPS, SLOTS, width), F32),
            pltpu.VMEM((STEPS * MOVES, width), F32),
            pltpu.SemaphoreType.DMA((3,)),
        ],
        compiler_params=params(VMEM_MOST),
        cost_estimate=cost(),
        name="pack_queries",
    )(moving, queries, fresh)


def released_kernel(*refs):
    del refs


def released(blocks, after):
    return pl.pallas_call(
        released_kernel,
        out_shape=[jax.ShapeDtypeStruct(block.shape, block.dtype) for block in blocks],
        in_specs=[ANY_SPEC] * (len(blocks) + len(after)),
        out_specs=[ANY_SPEC] * len(blocks),
        input_output_aliases={i: i for i in range(len(blocks))},
        cost_estimate=cost(),
        name="released",
    )(*blocks, *after)


def pack_kernel(moving_in, table_in, lengths_in, fresh_in, pool_in, *rest):
    (far, direct, both), rest = rest[:3], rest[3:]
    moving, table, lengths, fresh, pool, rows, sems = rest
    loads = fetch(
        (
            (moving_in, moving),
            (table_in, table),
            (lengths_in, lengths),
            (fresh_in, fresh),
            *parts_of(pool_in, pool),
        ),
        sems,
    )
    me = lax.axis_index("inst")
    for load in loads[:4]:
        load.wait()
    for step in range(STEPS):
        rows[step] = fresh[step].astype(F32)
    for load in loads[4:]:
        load.wait()
    for turn, target, start in ((0, far, 0), (2, both, 0), (1, both, MOVES)):
        for m in range(MOVES):
            slot = moving[turn, m, me]
            for page in range(PAGES):
                target[(start + m) * PAGES + page] = pool[table[0, slot * PAGES + page]]
        if turn == 0:
            direct[...] = far[FAR :]
        for step in range(turn):
            items = []
            for m in range(MOVES):
                slot = moving[turn, m, me]
                position = lengths[me, slot] + step
                items.append(
                    (
                        (start + m) * PAGES + lax.shift_right_logical(position, 4),
                        rows[step, pl.ds(slot, 1), :],
                        position & (TOKENS - 1),
                    )
                )
            put_tokens(target, items)


def pack(moving, table, lengths, fresh, pool):
    return pl.pallas_call(
        pack_kernel,
        out_shape=[
            jax.ShapeDtypeStruct((size,) + pool.shape[1:], BF16)
            for size in (MOVES * PAGES, MOVES * PAGES - FAR, 2 * MOVES * PAGES)
        ],
        in_specs=[HBM_SPEC] * 5,
        out_specs=[VMEM_SPEC] * 3,
        scratch_shapes=[
            pltpu.SMEM(moving.shape, jnp.int32),
            pltpu.SMEM(table.shape, jnp.int32),
            pltpu.SMEM(lengths.shape, jnp.int32),
            pltpu.VMEM(fresh.shape, BF16),
            pltpu.VMEM(pool.shape, BF16),
            pltpu.VMEM(fresh.shape, F32),
            pltpu.SemaphoreType.DMA((4 + CHUNKS,)),
        ],
        compiler_params=params(VMEM_MOST),
        cost_estimate=cost(),
        name="pack",
    )(moving, table, lengths, fresh, pool)


def gathered(pages, table, slot):
    return jnp.concatenate(
        [pages[table[0, slot * PAGES + page]] for page in range(PAGES)], axis=0
    )


def mark_slots(marks, moving, me):
    for slot in range(SLOTS):
        marks[slot] = STEPS
    for turn in range(STEPS):
        for m in range(MOVES):
            marks[moving[turn, m, me]] = turn


def serve_kernel(moving_in, table_in, lengths_in, *rest):
    asked_in, rest = rest[:STEPS], rest[STEPS:]
    queries_in, fresh_in, far, both, pool, weight, out, cache, *rest = rest
    moving, table, lengths, queries, fresh, *rest = rest
    asked, rest = rest[:STEPS], rest[STEPS:]
    pages, taken, weights, products, query, result, rows, asker, answer, row_list, packed, marks, *sems = rest
    me = lax.axis_index("inst")
    block = MOVES * PAGES
    width = GROUP * HEAD
    parts, rows_out, column = products.shape
    small_loads = fetch(
        (
            (moving_in, moving),
            (lengths_in, lengths),
            *zip(asked_in, asked),
            (table_in, table),
            (queries_in, queries),
            (fresh_in, fresh),
        ),
        sems[4],
    )
    moved_loads = fetch(
        (
            (far, taken.at[pl.ds(0, block)]),
            (both.at[pl.ds(block, block)], taken.at[pl.ds(block, block)]),
            (both.at[pl.ds(0, block)], taken.at[pl.ds(2 * block, block)]),
        ),
        sems[0],
    )
    pool_loads = fetch(parts_of(pool, pages), sems[1])
    weight_loads = fetch(
        [
            (weight.at[:, pl.ds(part * column, column)], weights.at[part])
            for part in range(parts)
        ],
        sems[2],
    )

    asker[...] = jnp.zeros_like(asker)
    query[...] = jnp.zeros_like(query)
    for load in small_loads:
        load.wait()
    counts = []
    for turn in range(STEPS):
        held = [lengths[me, moving[turn, m, me]] for m in range(MOVES)]
        counts += held
        moved_loads[turn].wait()
        for step in range(turn, STEPS):
            first = (step - turn) * MOVES
            row_list[...] = asked[turn][first : first + MOVES, :].astype(F32)
            for head in range(GROUP):
                asker[turn * MOVES : (turn + 1) * MOVES, step * GROUP + head, :] = row_list[
                    :, head * HEAD : (head + 1) * HEAD
                ]
            put_tokens(
                taken,
                [
                    (
                        turn * block + m * PAGES + lax.shift_right_logical(held[m] + step, 4),
                        row_list[m : m + 1, width:],
                        (held[m] + step) & (TOKENS - 1),
                    )
                    for m in range(MOVES)
                ],
            )
    values = attend_block(
        [
            taken[i * PAGES : (i + 1) * PAGES].reshape(PAGES * TOKENS, 2 * HEAD)
            for i in range(STEPS * MOVES)
        ],
        [asker[i].astype(BF16) for i in range(STEPS * MOVES)],
        counts,
    )
    for i, value in enumerate(values):
        answer[i] = value

    for step in range(STEPS):
        rows[step] = fresh[step].astype(F32)
        for head in range(GROUP):
            query[:, step * GROUP + head, :] = queries[
                step, :, head * HEAD : (head + 1) * HEAD
            ].astype(F32)
    mark_slots(marks, moving, me)
    for load in pool_loads:
        load.wait()

    @pl.loop(0, SLOTS // MOVES)
    def _(group):
        slots = [group * MOVES + m for m in range(MOVES)]
        held = [lengths[me, slot] for slot in slots]
        for step in range(STEPS):
            items = []
            for slot, length in zip(slots, held):
                position = length + step
                page = table[0, slot * PAGES + lax.shift_right_logical(position, 4)]
                items.append(
                    (page, rows[step, pl.ds(slot, 1), :], position & (TOKENS - 1))
                )
            put_tokens(pages, items)

    stores = fetch(parts_of(pages, cache), sems[1])

    @pl.loop(0, SLOTS // BATCH)
    def _(group):
        slots = [group * BATCH + m for m in range(BATCH)]
        values = attend_block(
            [gathered(pages, table, slot) for slot in slots],
            [query[slot].astype(BF16) for slot in slots],
            [lengths[me, slot] for slot in slots],
        )
        for slot, value in zip(slots, values):
            result[slot] = value

    start = 0
    for step in range(STEPS):
        natural = jnp.concatenate(
            [result[:, step * GROUP + head, :] for head in range(GROUP)], axis=1
        )
        row = start
        for slot in range(SLOTS):
            packed[pl.ds(row, 1), :] = natural[slot : slot + 1, :]
            row = row + (marks[slot] > step).astype(jnp.int32)
        start += KEPT[step]
    for turn in range(STEPS):
        for step in range(turn, STEPS):
            packed[start : start + MOVES, :] = jnp.concatenate(
                [
                    answer[turn * MOVES : (turn + 1) * MOVES, step * GROUP + head, :]
                    for head in range(GROUP)
                ],
                axis=1,
            )
            start += MOVES
    whole = packed[:start].astype(BF16)
    copies = []
    for part, load in enumerate(weight_loads):
        load.wait()
        products[part] = jnp.dot(
            whole, weights[part], preferred_element_type=F32
        ).astype(BF16)
        copies += fetch([(products.at[part], out.at[part])], sems[3].at[pl.ds(part, 1)])
    for copy in copies + stores:
        copy.wait()


def serve(moving, table, lengths, asked, queries, fresh, far, both, pool, weight, parts):
    page = pool.shape[1:]
    count = STEPS * MOVES
    kept_rows = sum(KEPT)
    depth, features = weight.shape
    column = features // parts
    total = kept_rows + sum(MOVED)
    return pl.pallas_call(
        serve_kernel,
        out_shape=[
            jax.ShapeDtypeStruct((parts, total, column), BF16),
            jax.ShapeDtypeStruct(pool.shape, BF16),
        ],
        in_specs=[ANY_SPEC] * (STEPS + 9),
        out_specs=[ANY_SPEC] * 2,
        scratch_shapes=[
            pltpu.SMEM(moving.shape, jnp.int32),
            pltpu.SMEM(table.shape, jnp.int32),
            pltpu.SMEM(lengths.shape, jnp.int32),
            pltpu.VMEM(queries.shape, BF16),
            pltpu.VMEM(fresh.shape, BF16),
            *[pltpu.VMEM(rows.shape, BF16) for rows in asked],
            pltpu.VMEM(pool.shape, BF16),
            pltpu.VMEM((count * PAGES,) + page, BF16),
            pltpu.VMEM((parts, depth, column), BF16),
            pltpu.VMEM((parts, total, column), BF16),
            pltpu.VMEM((SLOTS, ROWS, HEAD), F32),
            pltpu.VMEM((SLOTS, ROWS, HEAD), F32),
            pltpu.VMEM(fresh.shape, F32),
            pltpu.VMEM((count, ROWS, HEAD), F32),
            pltpu.VMEM((count, ROWS, HEAD), F32),
            pltpu.VMEM((MOVES, asked[0].shape[1]), F32),
            pltpu.VMEM((total + 8, depth), F32),
            pltpu.SMEM((SLOTS,), jnp.int32),
            pltpu.SemaphoreType.DMA((STEPS,)),
            pltpu.SemaphoreType.DMA((CHUNKS,)),
            pltpu.SemaphoreType.DMA((parts,)),
            pltpu.SemaphoreType.DMA((parts,)),
            pltpu.SemaphoreType.DMA((STEPS + 5,)),
        ],
        compiler_params=params(VMEM_MORE),
        cost_estimate=cost(),
        name="serve",
    )(moving, table, lengths, *asked, queries, fresh, far, both, pool, weight)


def insert_and_store(turn, hop, moving, table, lengths, rows, pages, cache, sem):
    me = lax.axis_index("inst")
    instances = lengths.shape[0]
    source = lax.rem(me - hop + instances, instances)
    slots = [moving[turn, m, me] for m in range(MOVES)]
    held = [lengths[source, moving[turn, m, source]] for m in range(MOVES)]
    for step in range(turn, STEPS):
        put_tokens(
            pages,
            [
                (
                    m * PAGES + lax.shift_right_logical(held[m] + step, 4),
                    rows[step, pl.ds(slots[m], 1), :],
                    (held[m] + step) & (TOKENS - 1),
                )
                for m in range(MOVES)
            ],
        )
    for m in range(MOVES):
        for page in range(PAGES):
            pltpu.make_async_copy(
                pages.at[m * PAGES + page],
                cache.at[table[0, slots[m] * PAGES + page]],
                sem,
            ).start()


def store_pages_kernel(turn, hop, moving, table, lengths, fresh, arrived, *rest):
    _, cache, *surplus, pages, rows, sem = rest
    for step in range(turn, STEPS):
        rows[step] = fresh[step].astype(F32)
    pages[...] = arrived[: MOVES * PAGES]
    insert_and_store(turn, hop, moving, table, lengths, rows, pages, cache, sem)
    for left in surplus:
        left[...] = arrived[MOVES * PAGES :]
    pltpu.make_async_copy(pages, cache.at[pl.ds(0, MOVES * PAGES)], sem).wait()


def store_pages(turn, hop, moving, table, lengths, fresh, arrived, cache):
    surplus = arrived.shape[0] - MOVES * PAGES
    return pl.pallas_call(
        functools.partial(store_pages_kernel, turn, hop),
        out_shape=[jax.ShapeDtypeStruct(cache.shape, BF16)]
        + [jax.ShapeDtypeStruct((surplus,) + cache.shape[1:], BF16)] * (surplus > 0),
        in_specs=[SMEM_SPEC] * 3 + [VMEM_SPEC] * 2 + [ANY_SPEC],
        out_specs=[ANY_SPEC] + [VMEM_SPEC] * (surplus > 0),
        scratch_shapes=[
            pltpu.VMEM((MOVES * PAGES,) + cache.shape[1:], BF16),
            pltpu.VMEM(fresh.shape, F32),
            pltpu.SemaphoreType.DMA,
        ],
        input_output_aliases={5: 0},
        compiler_params=params(),
        cost_estimate=cost(),
        name="store_pages",
    )(moving, table, lengths, fresh, arrived, cache)


def settle_kernel(moving, partial, direct, natural, *rest):
    outs, (kept, marks) = rest[:STEPS], rest[STEPS:]
    mark_slots(marks, moving, lax.axis_index("inst"))
    total = partial[0].astype(F32)
    for part in range(1, partial.shape[0]):
        total = total + partial[part].astype(F32)
    kept[...] = total
    row = 0
    for step in range(STEPS):
        index = row
        for slot in range(SLOTS):
            natural[step * SLOTS + slot : step * SLOTS + slot + 1, :] = kept[
                pl.ds(index, 1), :
            ]
            index = index + (marks[slot] > step).astype(jnp.int32)
        row += KEPT[step]
    for turn, out in enumerate(outs):
        value = kept[row : row + MOVED[turn]]
        row += MOVED[turn]
        if turn == 0:
            flat = jnp.concatenate([value[:, : 2 * HEAD], value[:, 2 * HEAD :]], axis=0)
            out[:LEAD] = flat.reshape(LEAD, TOKENS, 2 * HEAD).astype(BF16)
            out[LEAD:] = direct[...]
        else:
            out[...] = value.astype(BF16)


def settle(moving, partial, direct):
    _, rows, column = partial.shape
    out = pl.pallas_call(
        settle_kernel,
        out_shape=[jax.ShapeDtypeStruct((STEPS * SLOTS, column), F32)]
        + [jax.ShapeDtypeStruct((LEAD + direct.shape[0],) + direct.shape[1:], BF16)]
        + [jax.ShapeDtypeStruct((count, column), BF16) for count in MOVED[1:]],
        in_specs=[SMEM_SPEC] + [VMEM_SPEC] * 2,
        out_specs=[VMEM_SPEC] * (1 + STEPS),
        scratch_shapes=[
            pltpu.VMEM((rows, column), F32),
            pltpu.SMEM((SLOTS,), jnp.int32),
        ],
        compiler_params=params(),
        cost_estimate=cost(),
        name="settle",
    )(moving, partial, direct)
    return out[0], out[1:]


def finish_kernel(hop, moving, table, lengths, fresh, far, natural, *rest):
    taken, (_, out, cache, pages, rows, total, sem) = rest[:STEPS], rest[STEPS:]
    for step in range(STEPS):
        rows[step] = fresh[step].astype(F32)
    pages[: far.shape[0]] = far[...]
    pages[far.shape[0] :] = taken[0][LEAD:]
    insert_and_store(0, hop, moving, table, lengths, rows, pages, cache, sem)
    me = lax.axis_index("inst")
    total[...] = natural[...]
    for turn, block in enumerate(taken):
        if turn == 0:
            flat = block[:LEAD].astype(F32).reshape(LEAD * TOKENS, 2 * HEAD)
            values = jnp.concatenate([flat[: MOVED[0]], flat[MOVED[0] :]], axis=1)
        else:
            values = block[...].astype(F32)
        for step in range(turn, STEPS):
            for m in range(MOVES):
                k = (step - turn) * MOVES + m
                total[pl.ds(step * SLOTS + moving[turn, m, me], 1), :] = values[k : k + 1, :]
    out[...] = total[...].astype(BF16)
    pltpu.make_async_copy(pages, cache.at[pl.ds(0, MOVES * PAGES)], sem).wait()


def finish(hop, moving, table, lengths, fresh, far, natural, taken, cache):
    return pl.pallas_call(
        functools.partial(finish_kernel, hop),
        out_shape=[
            jax.ShapeDtypeStruct(natural.shape, BF16),
            jax.ShapeDtypeStruct(cache.shape, BF16),
        ],
        in_specs=[SMEM_SPEC] * 3 + [VMEM_SPEC] * (3 + STEPS) + [ANY_SPEC],
        out_specs=[VMEM_SPEC, ANY_SPEC],
        scratch_shapes=[
            pltpu.VMEM((MOVES * PAGES,) + cache.shape[1:], BF16),
            pltpu.VMEM(fresh.shape, F32),
            pltpu.VMEM(natural.shape, F32),
            pltpu.SemaphoreType.DMA,
        ],
        input_output_aliases={6 + STEPS: 1},
        compiler_params=params(),
        cost_estimate=cost(),
        name="finish",
    )(moving, table, lengths, fresh, far, natural, *taken, cache)


def shards(queries, incoming, pool, table, lengths, moving, weight):
    count = lax.axis_size("inst")
    parts = lax.axis_size("tp")
    hops = tuple(count // 2 ** (step + 1) for step in range(STEPS))
    fresh = incoming.reshape(STEPS, SLOTS, 2 * HEAD)
    own = pool.reshape(pool.shape[0], TOKENS, 2 * HEAD)

    moving = moving.transpose(0, 2, 1)
    block = MOVES * PAGES
    asked = pack_queries(moving, queries, fresh)
    asked = [shifted(rows, -hop) for rows, hop in zip(asked, hops)]
    far, direct, both = pack(moving, table, lengths, fresh, own)
    far, both = released((far, both), asked)
    both_in = shifted(both, hops[2])
    far_one = shifted(far, -hops[1])
    partial, cache = serve(
        moving, table, lengths, asked, queries, fresh, far, both, own, weight, parts
    )
    partial = lax.all_to_all(partial, "tp", 0, 0, tiled=True)
    common = (moving, table, lengths, fresh)
    cache, mid = store_pages(2, hops[2], *common, both_in, cache)
    mid_in = shifted(mid, hops[1] - hops[2])
    far_two = shifted(far_one[:FAR], -hops[2])
    far_in = shifted(far_two, -hops[2])
    natural, back = settle(moving, partial, direct)
    back = [shifted(rows, hop) for rows, hop in zip(back, hops)]
    (cache,) = store_pages(1, hops[1], *common, mid_in, cache)
    attended, cache = finish(hops[0], *common, far_in, natural, back, cache)
    return attended.reshape(queries.shape), cache.reshape(pool.shape)


def solution(mesh):
    placed = (
        P(None, "inst", "tp"),
        P(None, "inst", "tp", None),
        P("inst", "tp", None, None),
        P("inst", None),
        P(),
        P(),
        P("tp", None),
    )
    return jax.shard_map(
        shards,
        mesh=mesh,
        in_specs=placed,
        out_specs=(P(None, "inst", "tp"), P("inst", "tp", None, None)),
        check_vma=False,
    )
```
